768 devices in a mesh: row: 8 (over x, core), col: 8 (over y), basis: 12 (over z).
Axes of the slice: x: 4, y: 8, z: 12, core: 2. Of those that a mesh axis runs over, the one named last changes fastest.
Arguments:
- block_data: bfloat16 [6144, 128, 128], P(('row', 'col', 'basis')), may hold values from -1.1953125 to 1.1953125
- item_pairs: int32 [6144, 2], P(('row', 'col', 'basis')), may hold values from 0 to 1023
- dest_slot: int32 [6144], P(('row', 'col', 'basis')), may hold values from 0 to 63, as said below
- brick_tag: int32 [6144], P(('row', 'col', 'basis')), may hold values from 0 to 23
- centres: float32 [1024, 3, 128], replicated, may hold values from -1.5 to 1.5
- exponents: float32 [1024, 128], replicated, may hold values from 4 to 12
- levels: int32 [1536], replicated, may hold values 0 or 1
- cell_pos: int32 [1536, 256], P(('row', 'col', 'basis')), may hold values from 0 to 4095, as said below
- corner_refs: int32 [1536, 256, 8], P(('row', 'col', 'basis')), may hold values from 0 to 12287, as said below
Outputs:
- density: float32 [1536, 4096], P(('row', 'col', 'basis'))
The draws below stay inside these ranges and needn't reach their ends.
Inputs may be any that keep to these rules, and one draw needn't show every extreme that they name: `dest_slot`: on the rows of one device the values are distinct; value v sends the row to brick group v. `cell_pos`: within one brick the cells are distinct, one in each run of 16 consecutive points. `corner_refs`: index v names corner v % 8 of brick v // 8; every index occurs 256 times.
All inputs are finite; a program needn't handle non-finite values.
Results may differ from the reference program's by a relative error of at most 0.0028.
Values sent between devices are 32-bit elements; how exact they have to be, the bound alone decides.
A program may use at most 32 MiB of HBM per device.

```python
import math
import jax
import jax.numpy as jnp
from jax import lax

BS = 128
EDGE = 16
TC = 256
NBLK = 1024
ITEMS_DEV = 8
PTS = 4096
GROUPS = 64
CAP = 1
BRK_GRP = 24
BRICKS = 1536
ITEMS = 6144


def draw_dest_slot(key, part):
    device_total = ITEMS // ITEMS_DEV
    if ITEMS_DEV == GROUPS * CAP:

        def full_slots(index):
            return jax.random.permutation(jax.random.fold_in(key, index), GROUPS * CAP)
        slot_rows = jax.vmap(full_slots)(jnp.arange(device_total))
        return slot_rows.reshape(-1).astype(jnp.int32)
    popular_count = max(1, ITEMS_DEV // 2)
    band_width = max(1, device_total // 2)

    def pick_slots(index):
        band_index = index // band_width
        ranking = jax.random.permutation(jax.random.fold_in(key, 1000003 + band_index), GROUPS)
        popular = jnp.zeros((GROUPS,), jnp.int32).at[ranking[:popular_count]].set(1)
        jitter_draw = jax.random.randint(jax.random.fold_in(key, index), (GROUPS,), 0, 2 ** 14)
        own_group = (jnp.arange(GROUPS) == index % GROUPS).astype(jnp.int32)
        scores = own_group * 2 ** 26 + popular * 2 ** 22 + jitter_draw * GROUPS + jnp.arange(GROUPS)
        chosen = lax.top_k(scores, ITEMS_DEV)[1]
        shuffle = jax.random.permutation(jax.random.fold_in(key, 2000003 + index), ITEMS_DEV)
        return chosen[shuffle] * CAP
    slot_rows = jax.vmap(pick_slots)(jnp.arange(device_total))
    return slot_rows.reshape(-1).astype(jnp.int32)


def draw_cell_pos(key, part):
    stride_len = PTS // TC
    jitter_draw = jax.random.randint(key, (BRICKS, TC), 0, stride_len)
    jitter_draw = jitter_draw.at[0, 0].set(0).at[0, TC - 1].set(stride_len - 1)
    return (jnp.arange(TC)[None, :] * stride_len + jitter_draw).astype(jnp.int32)


def draw_corner_refs(key, part):
    mixed = jax.random.permutation(key, BRICKS * TC * 8)
    return (mixed % (BRICKS * 8)).reshape(BRICKS, TC, 8).astype(jnp.int32)


def plant(entries, key, low, top_value):
    place = [jax.random.randint(jax.random.fold_in(key, axis), (), 0, length) for axis, length in enumerate(entries.shape)]
    main_axis = entries.shape.index(max(entries.shape))
    beside = place[:main_axis] + [(place[main_axis] + 1) % entries.shape[main_axis]] + place[main_axis + 1:]
    return entries.at[tuple(place)].set(low).at[tuple(beside)].set(top_value)


def block_levels(own_key, dims, split, smallest, largest):
    def one(axis_at, blocks):
        heights = jax.random.uniform(jax.random.fold_in(jax.random.fold_in(own_key, 6), axis_at), (blocks,), jnp.float32, smallest / len(split), largest / len(split))
        return jnp.repeat(jnp.exp(heights), dims[axis_at] // blocks).reshape((-1,) + (1,) * (len(dims) - axis_at - 1))

    gain = one(*split[0])
    for cut in split[1:]:
        gain = gain * one(*cut)
    return gain


def scatter_about(key, shape, spread, limit, shards=(), kind=jnp.bfloat16):
    array = spread * jax.random.normal(key, shape, jnp.float32)
    if shards:
        array = array * block_levels(key, shape, shards, -0.22, 0.18)
    return jnp.clip(array, -limit, limit).astype(kind)


def setup_inputs(seed: int = 0) -> dict:
    arg_keys = jax.random.split(jax.random.key(seed), 10)
    block_data = scatter_about(arg_keys[0], (ITEMS, BS, BS), 0.2, 1.1953125, ((0, 768),))
    item_pairs = plant(jax.random.randint(arg_keys[1], (ITEMS, 2), 0, NBLK), jax.random.fold_in(arg_keys[1], 1), 0, NBLK - 1).astype(jnp.int32)
    dest_slot = draw_dest_slot(jax.random.fold_in(arg_keys[9], 71), 0)
    brick_tag = plant(jax.random.randint(arg_keys[3], (ITEMS,), 0, BRK_GRP), jax.random.fold_in(arg_keys[3], 1), 0, BRK_GRP - 1).astype(jnp.int32)
    centres = jnp.clip(jax.random.uniform(arg_keys[4], (NBLK, 3, BS), jnp.float32, -1.5, 1.5), -1.5, 1.5)
    exponents = jnp.clip(jnp.exp(jax.random.uniform(arg_keys[5], (NBLK, BS), jnp.float32, math.log(4.0), math.log(12.0))), 4.0, 12.0)
    levels = plant((jax.random.randint(arg_keys[6], (BRICKS,), 0, 4) < 3).astype(jnp.int32), jax.random.fold_in(arg_keys[6], 1), 0, 1)
    cell_pos = draw_cell_pos(jax.random.fold_in(arg_keys[9], 71), 0)
    corner_refs = draw_corner_refs(jax.random.fold_in(arg_keys[9], 71), 0)
    return {"block_data": block_data, "item_pairs": item_pairs, "dest_slot": dest_slot, "brick_tag": brick_tag, "centres": centres, "exponents": exponents, "levels": levels, "cell_pos": cell_pos, "corner_refs": corner_refs}


coarse_spacing = 0.2


def basis_values(centres, exponents, block_index, level_value, edge_points):
    spacing = coarse_spacing * jnp.exp2(-level_value.astype(jnp.float32))
    coords = (jnp.arange(edge_points, dtype=jnp.float32) - (edge_points - 1) / 2.0) * spacing
    middle = centres[block_index]
    decay_rates = exponents[block_index]
    factor = jnp.exp(-decay_rates[None, :, None] * (coords[None, None, :] - middle[:, :, None]) ** 2)
    values_grid = factor[0][:, :, None, None] * factor[1][:, None, :, None] * factor[2][:, None, None, :]
    return values_grid.reshape(decay_rates.shape[0], edge_points * edge_points * edge_points)


def pair_density(block_values, pair_index, level_value, centres, exponents, edge_points):
    row_values = basis_values(centres, exponents, pair_index[0], level_value, edge_points)
    col_values = basis_values(centres, exponents, pair_index[1], level_value, edge_points).astype(jnp.bfloat16)
    product = jnp.dot(block_values, col_values, preferred_element_type=jnp.float32)
    return jnp.sum(row_values * product, axis=0)


def corner_points(edge_points):
    corner_code = jnp.arange(8, dtype=jnp.int32)
    first = (corner_code // 4) * (edge_points - 1)
    second = ((corner_code // 2) % 2) * (edge_points - 1)
    third = (corner_code % 2) * (edge_points - 1)
    return ((first * edge_points + second) * edge_points + third).astype(jnp.int32)


def reference(block_data, item_pairs, dest_slot, brick_tag, centres, exponents, levels, cell_pos, corner_refs):
    target = ((dest_slot // CAP) * BRK_GRP + brick_tag).astype(jnp.int32)
    item_level = levels[target]

    def single(operands):
        return pair_density(operands[0], operands[1], operands[2], centres, exponents, EDGE)

    densities = lax.map(single, (block_data, item_pairs, item_level))
    brick_density = jax.ops.segment_sum(densities, target, num_segments=BRICKS)
    corner_values = brick_density[:, corner_points(EDGE)].reshape(-1)
    corner_mean = jnp.mean(corner_values[corner_refs], axis=-1)
    current = jnp.take_along_axis(brick_density, cell_pos, axis=1)
    brick_rows = jnp.arange(BRICKS, dtype=jnp.int32)[:, None]
    return brick_density.at[brick_rows, cell_pos].set(0.5 * current + 0.5 * corner_mean)
```

```python
import jax
import jax.numpy as jnp
from jax import lax
from jax.experimental import pallas as pl
from jax.experimental.pallas import tpu as pltpu
from jax.sharding import PartitionSpec as P

MESH = pl.DeviceIdType.MESH
F32 = jnp.float32
BF16 = jnp.bfloat16

EDGE = 16
HALF = (EDGE - 1) / 2.0
PTS = EDGE**3
BS = 128
ITEMS = 8
NR, NC, NZ = 8, 8, 12
GROUP = 24
SUB = 43
CHUNK = SUB * NC
WIDE = 384
ROWS = 48
NT = (((1,), (1,)), ((), ()))
CORNERS = tuple(
    ((c // 4) * 15 * EDGE + (c // 2 % 2) * 15) * EDGE + (c % 2) * 15 for c in range(8)
)


def lanes(shape):
    return lax.broadcasted_iota(jnp.int32, shape, len(shape) - 1)


def rows(shape):
    return lax.broadcasted_iota(jnp.int32, shape, len(shape) - 2)


def roll(x, shift):
    shift %= x.shape[-1]
    return x if shift == 0 else pltpu.roll(x, shift, x.ndim - 1)


def density_kernel(
    pairs_ref, slot_ref, tag_ref, levels_ref, cen_ref, exp_ref, block_ref, out_ref, dens_ref
):
    step16 = rows((EDGE, BS)).astype(F32) - HALF
    lane256 = lanes((1, EDGE * EDGE))
    step_y = (lane256 // EDGE).astype(F32) - HALF
    step_z = (lane256 % EDGE).astype(F32) - HALF
    step_x = lanes((1, BS)).astype(F32) - HALF
    dens_ref[:, PTS:] = jnp.zeros((ITEMS, dens_ref.shape[1] - PTS), F32)

    def item(k, targets):
        first, second = pairs_ref[0, k], pairs_ref[1, k]
        target = slot_ref[k] * GROUP + tag_ref[k]
        spacing = jnp.where(levels_ref[target] == 0, 0.2, 0.1).astype(F32)

        rate = exp_ref[pl.ds(second, 1), :]
        middle = [cen_ref[d, pl.ds(second, 1), :] for d in range(3)]
        col_x, col_y, col_z = [jnp.exp(-rate * (step16 * spacing - m) ** 2) for m in middle]
        col_yz = jnp.concatenate([col_y[y : y + 1] * col_z for y in range(EDGE)], axis=0)

        params = jnp.concatenate(
            [exp_ref[pl.ds(first, 1), :]]
            + [cen_ref[d, pl.ds(first, 1), :] for d in range(3)]
            + [jnp.zeros((4, BS), F32)],
            axis=0,
        )
        columns = jnp.transpose(params)
        decay = -columns[:, 0:1]
        row_x = jnp.exp(decay * (step_x * spacing - columns[:, 1:2]) ** 2)
        row_yz = jnp.exp(
            decay
            * (
                (step_y * spacing - columns[:, 2:3]) ** 2
                + (step_z * spacing - columns[:, 3:4]) ** 2
            )
        )
        block = block_ref[k]
        for x in range(EDGE):
            col_values = (col_x[x : x + 1] * col_yz).astype(BF16)
            product = lax.dot_general(block, col_values, NT, preferred_element_type=F32)
            weighted = product * row_yz * row_x[:, x : x + 1]
            dens_ref[pl.ds(k, 1), x * 256 : x * 256 + 256] = jnp.sum(
                weighted, axis=0, keepdims=True
            )
        return jnp.where(rows((ITEMS, BS)) == k, target.astype(F32), targets)

    targets = lax.fori_loop(0, ITEMS, item, jnp.zeros((ITEMS, BS), F32))

    lane = lanes((ITEMS, 128))
    base = CHUNK % 128
    extra = jnp.where(lane == base + 8, targets, 0.0)
    for c, q in enumerate(CORNERS):
        tile = dens_ref[:, q // 128 * 128 : q // 128 * 128 + 128]
        extra = jnp.where(lane == base + c, roll(tile, base + c - q), extra)
    for z in range(NZ):
        for j in range(WIDE // 128):
            start = z * CHUNK + j * 128
            tile, shift = start // 128, start % 128
            value = roll(dens_ref[:, tile * 128 : tile * 128 + 128], -shift)
            if shift:
                after = roll(dens_ref[:, tile * 128 + 128 : tile * 128 + 256], -shift)
                value = jnp.where(lane < 128 - shift, value, after)
            if j == CHUNK // 128:
                value = jnp.where(lane < base, value, extra)
            out_ref[z, :, j * 128 : j * 128 + 128] = value


def exchange_kernel(
    zs_ref,
    own_ref,
    tab_ref,
    z_got,
    turned,
    y_out,
    y_got,
    r_out,
    r_got,
    b_out,
    b_got,
    f_out,
    f_got,
    c_out,
    c_got,
    send_sem,
    recv_sem,
):
    me = {a: lax.axis_index(a) for a in ("row", "col", "basis")}
    size = {"row": NR, "col": NC, "basis": NZ}

    def device(axis, index):
        return tuple(index if a == axis else me[a] for a in ("row", "col", "basis"))

    barrier = pltpu.get_barrier_semaphore()
    for axis in ("basis", "col", "row"):
        for k in range(1, size[axis]):
            pl.semaphore_signal(
                barrier,
                inc=1,
                device_id=device(axis, lax.rem(me[axis] + k, size[axis])),
                device_id_type=MESH,
            )
    pl.semaphore_wait(barrier, NR + NC + NZ - 3)

    def start(axis, out, got, stage, each):
        copies = []
        for k in range(1, size[axis]):
            to = lax.rem(me[axis] + k, size[axis])
            copy = pltpu.make_async_remote_copy(
                src_ref=out.at[to] if each else out,
                dst_ref=got.at[me[axis]],
                send_sem=send_sem.at[stage, k],
                recv_sem=recv_sem.at[stage, k],
                device_id=device(axis, to),
                device_id_type=MESH,
            )
            copy.start()
            copies.append(copy)
        got[me[axis]] = out[me[axis]] if each else out[...]
        return copies

    def arrive(copies):
        for copy in copies:
            copy.wait_recv()

    lane = lanes((24, 128))

    z_copies = start("basis", zs_ref, z_got, 0, True)
    arrive(z_copies)
    held = jnp.concatenate(
        [z_got[...].reshape(NZ * ITEMS, WIDE), jnp.zeros((128 - NZ * ITEMS, WIDE), F32)], axis=0
    )
    turned[...] = jnp.transpose(held)

    row = rows((ROWS, 128))
    for y in range(NC):
        slab = turned[y * SUB : y * SUB + ROWS, :]
        corner = turned[CHUNK + y : CHUNK + y + 1, :]
        target = turned[CHUNK + 8 : CHUNK + 9, :]
        y_out[y] = jnp.where(row < SUB, slab, jnp.where(row == SUB, corner, target))
    y_copies = start("col", y_out, y_got, 1, True)
    arrive(y_copies)

    pieces = []
    targets = []
    for y in range(NC):
        value = y_got[y]
        high = value.astype(BF16)
        low = (value - high.astype(F32)).astype(BF16)
        pieces.append(jnp.concatenate([high, low], axis=0))
        targets.append(y_got[y, SUB + 1 : SUB + 2, :])
    left = jnp.concatenate(pieces, axis=1)
    brick = rows((128, 128)).astype(F32)

    def table(base, upper):
        number = brick + float(base)
        if upper:
            number = number + jnp.where(brick >= 64.0, float(upper), 0.0)
        right = jnp.concatenate(
            [jnp.where(number == t, 1.0, 0.0).astype(BF16) for t in targets], axis=1
        )
        both = lax.dot_general(left, right, NT, preferred_element_type=F32)
        return both[:ROWS] + both[ROWS:]

    for j in range(NR // 2):
        r_out[2 * j, :ROWS] = table(384 * j, 0)
        r_out[2 * j + 1, :ROWS] = table(384 * j + 192, 0)
        mixed = table(384 * j + 128, 128)
        upper, lower = mixed[:24], mixed[24:]
        r_out[2 * j, ROWS:] = jnp.where(lane < 64, upper, roll(lower, 64))
        r_out[2 * j + 1, ROWS:] = jnp.where(lane < 64, roll(upper, 64), lower)

    r_copies = start("row", r_out, r_got, 2, True)
    arrive(r_copies)
    total = r_got[0]
    for r in range(1, NR):
        total = total + r_got[r]
    head, tail = total[:ROWS], total[ROWS:]
    tail = jnp.concatenate([tail, roll(tail, 64)], axis=0)
    both = jnp.concatenate([head, tail], axis=1)
    bricks = jnp.transpose(jnp.concatenate([both, jnp.zeros((128 - ROWS, 256), F32)], axis=0))

    corner_rows = jnp.concatenate(
        [head[SUB : SUB + 1], tail[SUB : SUB + 1], jnp.zeros((6, 128), F32)], axis=0
    )
    for y in range(NC):
        b_out[y, :GROUP] = bricks[y * GROUP : y * GROUP + GROUP]
        b_out[y, GROUP:] = corner_rows
    b_copies = start("col", b_out, b_got, 3, True)
    arrive(b_copies)

    for y in range(NC):
        c_out[y : y + 1, :128] = b_got[y, GROUP : GROUP + 1, :]
        c_out[y : y + 1, 128:] = b_got[y, GROUP + 1 : GROUP + 2, :]
    c_copies = start("row", c_out, c_got, 4, False)

    for j in range(WIDE // 128):
        value = jnp.zeros((GROUP, 128), F32)
        for y in range(NC):
            first, last = y * SUB - j * 128, (y + 1) * SUB - j * 128
            if first < 128 and last > 0:
                moved = roll(b_got[y, :GROUP], first)
                value = jnp.where((lane >= first) & (lane < last), moved, value)
        for z in range(NZ):
            f_out[z, :, j * 128 : j * 128 + 128] = value[2 * z : 2 * z + 2]
    f_copies = start("basis", f_out, f_got, 5, True)
    arrive(f_copies)
    lane2 = lanes((2, 128))
    for t in range(PTS // 128):
        value = None
        for z in range(NZ):
            first, last = z * CHUNK - t * 128, (z + 1) * CHUNK - t * 128
            if first < 128 and last > 0:
                tile, shift = (-first) // 128, (-first) % 128
                part = None
                for at in (tile, tile + 1):
                    low = at * 128 + first
                    if 0 <= at < WIDE // 128 and low < 128 and low + 128 > 0:
                        moved = roll(f_got[z, :, at * 128 : at * 128 + 128], low)
                        part = moved if part is None else jnp.where(lane2 < low, part, moved)
                value = part if value is None else jnp.where(lane2 < first, value, part)
        own_ref[:, t * 128 : t * 128 + 128] = value
    arrive(c_copies)
    tab_ref[...] = c_got[...]
    for copies in (z_copies, y_copies, r_copies, b_copies, c_copies, f_copies):
        for copy in copies:
            copy.wait_send()


def finish_kernel(own_ref, tab_ref, refs_ref, cell_ref, out_ref):
    for b in range(2):
        means = []
        for h in range(2):
            ref = refs_ref[b, :, h * 128 : h * 128 + 128]
            corner, brick = ref & 7, ref >> 3
            source = ((brick >> 6) * 11) >> 5
            place = brick - source * 192
            at = place & 127
            which = (source * 2 + (place >> 7)) * 8 + corner
            found = jnp.zeros((8, 128), F32)
            for r in range(NR):
                for half in range(2):
                    for c in range(8):
                        line = jnp.broadcast_to(
                            tab_ref[r, c : c + 1, half * 128 : half * 128 + 128], (8, 128)
                        )
                        here = jnp.take_along_axis(line, at, axis=1)
                        found = jnp.where(which == (r * 2 + half) * 8 + c, here, found)
            means.append(jnp.sum(found, axis=0, keepdims=True) * 0.0625)
        mean = jnp.concatenate(means, axis=1)
        cell = cell_ref[b : b + 1, :]
        upper = rows((32, 256)) == (cell >> 7)
        high = mean.astype(BF16).astype(F32)
        left = jnp.concatenate(
            [
                jnp.where(upper, high, 0.0),
                jnp.where(upper, mean - high, 0.0),
                jnp.where(upper, 0.5, 0.0),
            ],
            axis=0,
        ).astype(BF16)
        right = jnp.where(rows((128, 256)) == (cell & 127), 1.0, 0.0).astype(BF16)
        spread = lax.dot_general(left, right, NT, preferred_element_type=F32)
        added, kept = spread[:32] + spread[32:64], 1.0 - spread[64:]
        for t in range(PTS // 128):
            part = slice(t * 128, t * 128 + 128)
            out_ref[b : b + 1, part] = (
                own_ref[b : b + 1, part] * kept[t : t + 1] + added[t : t + 1]
            )


def body(
    block_data, item_pairs, dest_slot, brick_tag, centres, exponents, levels, cell_pos, corner_refs
):
    vmem = pl.BlockSpec(memory_space=pltpu.VMEM)
    smem = pl.BlockSpec(memory_space=pltpu.SMEM)
    chunks = pl.pallas_call(
        density_kernel,
        out_shape=jax.ShapeDtypeStruct((NZ, ITEMS, WIDE), F32),
        in_specs=[smem] * 4 + [vmem] * 3,
        out_specs=vmem,
        scratch_shapes=[pltpu.VMEM((ITEMS, 34 * 128), F32)],
        compiler_params=pltpu.CompilerParams(vmem_limit_bytes=32 * 2**20),
        name="pair_density",
    )(
        item_pairs.T,
        dest_slot,
        brick_tag,
        levels,
        centres.transpose(1, 0, 2),
        exponents,
        block_data,
    )
    own, corners = pl.pallas_call(
        exchange_kernel,
        out_shape=(
            jax.ShapeDtypeStruct((2, PTS), F32),
            jax.ShapeDtypeStruct((NR, 8, 256), F32),
        ),
        in_specs=[vmem],
        out_specs=(vmem, vmem),
        scratch_shapes=[
            pltpu.VMEM((NZ, ITEMS, WIDE), F32),
            pltpu.VMEM((WIDE, 128), F32),
            pltpu.VMEM((NC, ROWS, 128), F32),
            pltpu.VMEM((NC, ROWS, 128), F32),
            pltpu.VMEM((NR, ROWS + 24, 128), F32),
            pltpu.VMEM((NR, ROWS + 24, 128), F32),
            pltpu.VMEM((NC, GROUP + 8, 128), F32),
            pltpu.VMEM((NC, GROUP + 8, 128), F32),
            pltpu.VMEM((NZ, 2, WIDE), F32),
            pltpu.VMEM((NZ, 2, WIDE), F32),
            pltpu.VMEM((8, 256), F32),
            pltpu.VMEM((NR, 8, 256), F32),
            pltpu.SemaphoreType.DMA((6, NZ)),
            pltpu.SemaphoreType.DMA((6, NZ)),
        ],
        compiler_params=pltpu.CompilerParams(
            collective_id=0, has_side_effects=True, vmem_limit_bytes=32 * 2**20
        ),
        name="exchange",
    )(chunks)
    return pl.pallas_call(
        finish_kernel,
        out_shape=jax.ShapeDtypeStruct((2, PTS), F32),
        in_specs=[vmem] * 4,
        out_specs=vmem,
        compiler_params=pltpu.CompilerParams(vmem_limit_bytes=32 * 2**20),
        name="cells",
    )(own, corners, corner_refs.transpose(0, 2, 1), cell_pos)


def solution(mesh):
    spread = ("row", "col", "basis")
    return jax.shard_map(
        body,
        mesh=mesh,
        in_specs=(
            P(spread, None, None),
            P(spread, None),
            P(spread),
            P(spread),
            P(),
            P(),
            P(),
            P(spread, None),
            P(spread, None, None),
        ),
        out_specs=P(spread, None),
        check_vma=False,
    )
```

```python
import itertools

import jax
import jax.numpy as jnp
from jax import lax
from jax.experimental import pallas as pl
from jax.experimental.pallas import tpu as pltpu
from jax.sharding import PartitionSpec as P

MESH = pl.DeviceIdType.MESH
F32 = jnp.float32
BF16 = jnp.bfloat16

EDGE = 16
HALF = (EDGE - 1) / 2.0
PTS = EDGE**3
BS = 128
ITEMS = 8
NR, NC, NZ = 8, 8, 12
PLANE = NC * NZ
GROUP = 24
OWN = NC * GROUP
SUB = 43
TARGET = SUB
CORNER = 48
ROWS = 56
NT = (((1,), (1,)), ((), ()))
CORNERS = tuple(
    ((c // 4) * 15 * EDGE + (c // 2 % 2) * 15) * EDGE + (c % 2) * 15 for c in range(8)
)


def far(step, size):
    return min(step, size - step)


PLANE_STEPS = sorted(
    (s for s in itertools.product(range(NC), range(NZ)) if any(s)),
    key=lambda s: -(far(s[0], NC) + far(s[1], NZ)),
)
ROW_STEPS = ((2, 1), (2, 0), (1, 1), (3, 1), (1, 0), (3, 0), (0, 1))


def lanes(shape):
    return lax.broadcasted_iota(jnp.int32, shape, len(shape) - 1)


def rows(shape):
    return lax.broadcasted_iota(jnp.int32, shape, len(shape) - 2)


def roll(x, shift):
    shift %= x.shape[-1]
    return x if shift == 0 else pltpu.roll(x, shift, x.ndim - 1)


def kernel(
    pairs_hbm,
    slot_hbm,
    tag_hbm,
    levels_hbm,
    cen_hbm,
    exp_hbm,
    block_hbm,
    refs_hbm,
    cell_hbm,
    out_ref,
    pairs_ref,
    slot_ref,
    tag_ref,
    levels_ref,
    cen_ref,
    exp_ref,
    block_ref,
    refs_ref,
    cell_ref,
    dens_ref,
    a_out,
    a_got,
    r_out,
    r_got,
    b_out,
    b_got,
    c_out,
    c_got,
    load_sem,
    again_sem,
    a_send,
    a_recv,
    r_send,
    r_recv,
    b_send,
    b_recv,
    c_send,
    c_recv,
):
    loads = [
        pltpu.make_async_copy(source, into, load_sem.at[n])
        for n, (source, into) in enumerate(
            (
                (pairs_hbm, pairs_ref),
                (slot_hbm, slot_ref),
                (tag_hbm, tag_ref),
                (levels_hbm, levels_ref),
                (cen_hbm, cen_ref),
                (exp_hbm, exp_ref),
                (block_hbm, block_ref),
                (refs_hbm, refs_ref),
                (cell_hbm, cell_ref),
            )
        )
    ]
    for load in loads:
        load.start()

    r, y, z = (lax.axis_index(a) for a in ("row", "col", "basis"))
    ys = [lax.rem(y + n, NC) for n in range(NC)]
    zs = [lax.rem(z + n, NZ) for n in range(NZ)]
    x, core = r // 2, lax.rem(r, 2)
    xs = [lax.rem(x + n, NR // 2) * 2 for n in range(NR // 2)]
    cores = [core, 1 - core]
    row_of = [xs[dx] + cores[dc] for dx, dc in ROW_STEPS]
    me = y * NZ + z

    barrier = pltpu.get_barrier_semaphore()
    for n in range(1, NZ):
        pl.semaphore_signal(barrier, inc=1, device_id=(r, y, zs[n]), device_id_type=MESH)
    for n in range(1, NC):
        pl.semaphore_signal(barrier, inc=1, device_id=(r, ys[n], z), device_id_type=MESH)
    for other in row_of:
        pl.semaphore_signal(barrier, inc=1, device_id=(other, y, z), device_id_type=MESH)

    step16 = rows((EDGE, BS)).astype(F32) - HALF
    lane256 = lanes((1, EDGE * EDGE))
    step_y = (lane256 // EDGE).astype(F32) - HALF
    step_z = (lane256 % EDGE).astype(F32) - HALF
    step_x = lanes((1, BS)).astype(F32) - HALF
    dens_ref[:, PTS:] = jnp.zeros((ITEMS, dens_ref.shape[1] - PTS), F32)
    for load in loads:
        load.wait()

    def item(k, targets):
        first, second = pairs_ref[0, k], pairs_ref[1, k]
        group, tag = slot_ref[k], tag_ref[k]
        spacing = jnp.where(levels_ref[group * GROUP + tag] == 0, 0.2, 0.1).astype(F32)

        rate = exp_ref[pl.ds(second, 1), :]
        middle = [cen_ref[d, pl.ds(second, 1), :] for d in range(3)]
        col_x, col_y, col_z = [jnp.exp(-rate * (step16 * spacing - m) ** 2) for m in middle]
        col_yz = jnp.concatenate([col_y[n : n + 1] * col_z for n in range(EDGE)], axis=0)

        params = jnp.concatenate(
            [exp_ref[pl.ds(first, 1), :]]
            + [cen_ref[d, pl.ds(first, 1), :] for d in range(3)]
            + [jnp.zeros((4, BS), F32)],
            axis=0,
        )
        columns = jnp.transpose(params)
        decay = -columns[:, 0:1]
        row_x = jnp.exp(decay * (step_x * spacing - columns[:, 1:2]) ** 2)
        row_yz = jnp.exp(
            decay
            * (
                (step_y * spacing - columns[:, 2:3]) ** 2
                + (step_z * spacing - columns[:, 3:4]) ** 2
            )
        )
        block = block_ref[k]
        for n in range(EDGE):
            col_values = (col_x[n : n + 1] * col_yz).astype(BF16)
            product = lax.dot_general(block, col_values, NT, preferred_element_type=F32)
            weighted = product * row_yz * row_x[:, n : n + 1]
            dens_ref[pl.ds(k, 1), n * 256 : n * 256 + 256] = jnp.sum(
                weighted, axis=0, keepdims=True
            )
        place = (group & 7) * GROUP + tag
        number = (group >> 3) * OWN + (place & 1) * PLANE + (place >> 1)
        return jnp.where(rows((ITEMS, 128)) == k, number.astype(F32), targets)

    numbers = lax.fori_loop(0, ITEMS // 2, item, jnp.zeros((ITEMS, 128), F32))
    pl.semaphore_wait(barrier, NR + NC + NZ - 3)
    for n in range(1, NC):
        pl.semaphore_signal(again_sem, inc=1, device_id=(r, ys[n], z), device_id_type=MESH)
    numbers = lax.fori_loop(ITEMS // 2, ITEMS, item, numbers)

    lane = lanes((ITEMS, 128))
    extra = jnp.where(lane == TARGET, numbers, 0.0)
    for c, q in enumerate(CORNERS):
        tile = dens_ref[:, q // 128 * 128 : q // 128 * 128 + 128]
        extra = jnp.where(lane == CORNER + c, roll(tile, CORNER + c - q), extra)
    half = lanes((4, 128)) < 64
    for a in range(PLANE):
        tile, shift = a * SUB // 128, a * SUB % 128
        value = roll(dens_ref[:, tile * 128 : tile * 128 + 128], -shift)
        if shift + SUB > 128:
            after = roll(dens_ref[:, tile * 128 + 128 : tile * 128 + 256], -shift)
            value = jnp.where(lane < 128 - shift, value, after)
        value = jnp.where(lane < SUB, value, extra)
        a_out[a] = jnp.where(half, value[:4], roll(value, 64)[4:])
    pl.semaphore_wait(again_sem, NC - 1)

    def plane_copies(out, got, send, recv):
        return [
            pltpu.make_async_remote_copy(
                src_ref=out.at[ys[dy] * NZ + zs[dz]],
                dst_ref=got.at[me],
                send_sem=send.at[n],
                recv_sem=recv.at[n],
                device_id=(r, ys[dy], zs[dz]),
                device_id_type=MESH,
            )
            for n, (dy, dz) in enumerate(PLANE_STEPS)
        ]

    a_copies = plane_copies(a_out, a_got, a_send, a_recv)
    for copy in a_copies:
        copy.start()
    a_got[me] = a_out[me]
    for copy in a_copies:
        copy.wait_recv()

    turned = jnp.transpose(
        jnp.concatenate([a_got[a] for a in range(PLANE)], axis=0)
    )
    values = jnp.concatenate([turned[:ROWS], turned[64 : 64 + ROWS]], axis=1)
    high = values.astype(BF16)
    low = (values - high.astype(F32)).astype(BF16)
    left = jnp.concatenate([high, low], axis=0)
    wanted = values[TARGET : TARGET + 1, :]
    count = rows((128, PLANE * ITEMS)).astype(F32)
    count2 = jnp.where(count < 64.0, count + 128.0, count + 64.0)
    half = lanes((32, 128)) < 64

    def table(row):
        here = wanted - (row * OWN).astype(F32)
        parts = []
        for at in (count, count2):
            right = jnp.where(at == here, 1.0, 0.0).astype(BF16)
            both = lax.dot_general(left, right, NT, preferred_element_type=F32)
            parts.append(both[:ROWS] + both[ROWS:])
        whole, mixed = parts
        mixed = jnp.concatenate([mixed, jnp.zeros((64 - ROWS, 128), F32)], axis=0)
        return jnp.concatenate([whole, jnp.where(half, mixed[:32], mixed[32:])], axis=0)

    r_copies = []
    for n, other in enumerate(row_of):
        r_out[n] = table(other)
        copy = pltpu.make_async_remote_copy(
            src_ref=r_out.at[n],
            dst_ref=r_got.at[n],
            send_sem=r_send.at[n],
            recv_sem=r_recv.at[n],
            device_id=(other, y, z),
            device_id_type=MESH,
        )
        copy.start()
        r_copies.append(copy)
    total = table(r)
    for n, copy in enumerate(r_copies):
        copy.wait_recv()
        total = total + r_got[n]
    whole, mixed = total[:ROWS], total[ROWS:]
    mixed = jnp.concatenate([mixed, roll(mixed, 64)], axis=0)
    c_out[:, :128] = whole[CORNER : CORNER + 8]
    c_out[:, 128:] = mixed[CORNER : CORNER + 8]

    c_copies = [
        pltpu.make_async_remote_copy(
            src_ref=c_out,
            dst_ref=c_got.at[r],
            send_sem=c_send.at[n],
            recv_sem=c_recv.at[n],
            device_id=(other, y, z),
            device_id_type=MESH,
        )
        for n, other in enumerate(row_of)
    ]
    for copy in c_copies:
        copy.start()
    c_got[r] = c_out[...]

    whole = jnp.concatenate([whole, jnp.zeros((64 - ROWS, 128), F32)], axis=0)
    second = jnp.where(lanes((64, 128)) < 32, roll(whole, 32), roll(mixed, 32))
    bricks = jnp.transpose(jnp.concatenate([whole, second], axis=0))
    for a in range(PLANE):
        b_out[a] = bricks[a : a + 1]
    b_copies = plane_copies(b_out, b_got, b_send, b_recv)
    for copy in b_copies:
        copy.start()
    b_got[me] = b_out[me]

    for copy in c_copies:
        copy.wait_recv()
    kept, added = [], []
    for b in range(2):
        means = []
        for h in range(2):
            ref = refs_ref[b, :, h * 128 : h * 128 + 128]
            corner, brick = ref & 7, ref >> 3
            source = ((brick >> 6) * 11) >> 5
            place = brick - source * OWN
            place = (place >> 1) + (place & 1) * PLANE
            at = place & 127
            which = (source * 2 + (place >> 7)) * 8 + corner
            found = jnp.zeros((8, 128), F32)
            for n in range(NR):
                for part in range(2):
                    for c in range(8):
                        line = jnp.broadcast_to(
                            c_got[n, c : c + 1, part * 128 : part * 128 + 128], (8, 128)
                        )
                        here = jnp.take_along_axis(line, at, axis=1)
                        found = jnp.where(which == (n * 2 + part) * 8 + c, here, found)
            means.append(jnp.sum(found, axis=0, keepdims=True) * 0.0625)
        mean = jnp.concatenate(means, axis=1)
        cell = cell_ref[b : b + 1, :]
        upper = rows((32, 256)) == (cell >> 7)
        coarse = mean.astype(BF16).astype(F32)
        weights = jnp.concatenate(
            [
                jnp.where(upper, coarse, 0.0),
                jnp.where(upper, mean - coarse, 0.0),
                jnp.where(upper, 0.5, 0.0),
            ],
            axis=0,
        ).astype(BF16)
        spots = jnp.where(rows((128, 256)) == (cell & 127), 1.0, 0.0).astype(BF16)
        spread = lax.dot_general(weights, spots, NT, preferred_element_type=F32)
        added.append(spread[:32] + spread[32:64])
        kept.append(1.0 - spread[64:])

    for copy in b_copies:
        copy.wait_recv()
    lane = lanes((1, 128))
    for b in range(2):
        for t in range(PTS // 128):
            value = None
            for a in range(PLANE):
                first = a * SUB - t * 128
                if first < 128 and first + SUB > 0:
                    moved = roll(b_got[a], first - 64 * b)
                    value = moved if value is None else jnp.where(lane < first, value, moved)
            out_ref[b : b + 1, t * 128 : t * 128 + 128] = (
                value * kept[b][t : t + 1] + added[b][t : t + 1]
            )
    for copies in (a_copies, r_copies, b_copies, c_copies):
        for copy in copies:
            copy.wait_send()


def body(
    block_data, item_pairs, dest_slot, brick_tag, centres, exponents, levels, cell_pos, corner_refs
):
    arguments = (
        item_pairs.T,
        dest_slot,
        brick_tag,
        levels,
        centres.transpose(1, 0, 2),
        exponents,
        block_data,
        corner_refs.transpose(0, 2, 1),
        cell_pos,
    )
    places = [pltpu.SMEM] * 4 + [pltpu.VMEM] * 5
    dma = pltpu.SemaphoreType.DMA
    return pl.pallas_call(
        kernel,
        out_shape=jax.ShapeDtypeStruct((2, PTS), F32),
        in_specs=[pl.BlockSpec(memory_space=pltpu.HBM)] * len(arguments),
        out_specs=pl.BlockSpec(memory_space=pltpu.VMEM),
        scratch_shapes=[place(a.shape, a.dtype) for place, a in zip(places, arguments)]
        + [
            pltpu.VMEM((ITEMS, 34 * 128), F32),
            pltpu.VMEM((PLANE, 4, 128), F32),
            pltpu.VMEM((PLANE, 4, 128), F32),
            pltpu.VMEM((NR - 1, ROWS + 32, 128), F32),
            pltpu.VMEM((NR - 1, ROWS + 32, 128), F32),
            pltpu.VMEM((PLANE, 1, 128), F32),
            pltpu.VMEM((PLANE, 1, 128), F32),
            pltpu.VMEM((8, 256), F32),
            pltpu.VMEM((NR, 8, 256), F32),
            dma((len(arguments),)),
            pltpu.SemaphoreType.REGULAR,
            dma((PLANE - 1,)),
            dma((PLANE - 1,)),
            dma((NR - 1,)),
            dma((NR - 1,)),
            dma((PLANE - 1,)),
            dma((PLANE - 1,)),
            dma((NR - 1,)),
            dma((NR - 1,)),
        ],
        compiler_params=pltpu.CompilerParams(
            collective_id=0, has_side_effects=True, vmem_limit_bytes=60 * 2**20
        ),
        name="collocate",
    )(*arguments)


def solution(mesh):
    spread = ("row", "col", "basis")
    return jax.shard_map(
        body,
        mesh=mesh,
        in_specs=(
            P(spread, None, None),
            P(spread, None),
            P(spread),
            P(spread),
            P(),
            P(),
            P(),
            P(spread, None),
            P(spread, None, None),
        ),
        out_specs=P(spread, None),
        check_vma=False,
    )
```

```python
import itertools

import jax
import jax.numpy as jnp
from jax import lax
from jax.experimental import pallas as pl
from jax.experimental.pallas import tpu as pltpu
from jax.sharding import PartitionSpec as P

MESH = pl.DeviceIdType.MESH
F32 = jnp.float32
BF16 = jnp.bfloat16

EDGE = 16
HALF = (EDGE - 1) / 2.0
PTS = EDGE**3
BS = 128
ITEMS = 8
NR, NC, NZ = 8, 8, 12
PLANE = NC * NZ
GROUP = 24
OWN = NC * GROUP
SUB = 43
TARGET = SUB
CORNER = 48
ROWS = 56
NT = (((1,), (1,)), ((), ()))
CORNERS = tuple(
    ((c // 4) * 15 * EDGE + (c // 2 % 2) * 15) * EDGE + (c % 2) * 15 for c in range(8)
)


def far(step, size):
    return min(step, size - step)


PLANE_STEPS = sorted(
    (s for s in itertools.product(range(NC), range(NZ)) if any(s)),
    key=lambda s: -(far(s[0], NC) + far(s[1], NZ)),
)
ROW_STEPS = ((2, 1), (2, 0), (1, 1), (3, 1), (1, 0), (3, 0), (0, 1))


def lanes(shape):
    return lax.broadcasted_iota(jnp.int32, shape, len(shape) - 1)


def rows(shape):
    return lax.broadcasted_iota(jnp.int32, shape, len(shape) - 2)


def roll(x, shift):
    shift %= x.shape[-1]
    return x if shift == 0 else pltpu.roll(x, shift, x.ndim - 1)


def kernel(
    pairs_hbm,
    slot_hbm,
    tag_hbm,
    levels_hbm,
    cen_hbm,
    exp_hbm,
    block_hbm,
    refs_hbm,
    cell_hbm,
    out_ref,
    pairs_ref,
    slot_ref,
    tag_ref,
    levels_ref,
    cen_ref,
    exp_ref,
    block_ref,
    refs_ref,
    cell_ref,
    dens_ref,
    a_out,
    a_got,
    r_out,
    r_got,
    b_out,
    b_got,
    c_out,
    c_got,
    load_sem,
    again_sem,
    a_send,
    a_recv,
    r_send,
    r_recv,
    b_send,
    b_recv,
    c_send,
    c_recv,
):
    loads = [
        pltpu.make_async_copy(source, into, load_sem.at[n])
        for n, (source, into) in enumerate(
            (
                (pairs_hbm, pairs_ref),
                (slot_hbm, slot_ref),
                (tag_hbm, tag_ref),
                (levels_hbm, levels_ref),
                (cen_hbm, cen_ref),
                (exp_hbm, exp_ref),
                (block_hbm, block_ref),
                (refs_hbm, refs_ref),
                (cell_hbm, cell_ref),
            )
        )
    ]
    for load in loads:
        load.start()

    r, y, z = (lax.axis_index(a) for a in ("row", "col", "basis"))
    ys = [lax.rem(y + n, NC) for n in range(NC)]
    zs = [lax.rem(z + n, NZ) for n in range(NZ)]
    x, core = r // 2, lax.rem(r, 2)
    xs = [lax.rem(x + n, NR // 2) * 2 for n in range(NR // 2)]
    cores = [core, 1 - core]
    row_of = [xs[dx] + cores[dc] for dx, dc in ROW_STEPS]
    me = y * NZ + z

    barrier = pltpu.get_barrier_semaphore()
    for n in range(1, NZ):
        pl.semaphore_signal(barrier, inc=1, device_id=(r, y, zs[n]), device_id_type=MESH)
    for n in range(1, NC):
        pl.semaphore_signal(barrier, inc=1, device_id=(r, ys[n], z), device_id_type=MESH)
    for other in row_of:
        pl.semaphore_signal(barrier, inc=1, device_id=(other, y, z), device_id_type=MESH)

    step16 = rows((EDGE, BS)).astype(F32) - HALF
    lane256 = lanes((1, EDGE * EDGE))
    step_y = (lane256 // EDGE).astype(F32) - HALF
    step_z = (lane256 % EDGE).astype(F32) - HALF
    step_x = lanes((1, BS)).astype(F32) - HALF
    for load in loads:
        load.wait()

    def item(k, targets):
        first, second = pairs_ref[0, k], pairs_ref[1, k]
        group, tag = slot_ref[k], tag_ref[k]
        spacing = jnp.where(levels_ref[group * GROUP + tag] == 0, 0.2, 0.1).astype(F32)

        rate = exp_ref[pl.ds(second, 1), :]
        middle = [cen_ref[d, pl.ds(second, 1), :] for d in range(3)]
        col_x, col_y, col_z = [jnp.exp(-rate * (step16 * spacing - m) ** 2) for m in middle]
        col_yz = jnp.concatenate([col_y[n : n + 1] * col_z for n in range(EDGE)], axis=0)

        params = jnp.concatenate(
            [exp_ref[pl.ds(first, 1), :]]
            + [cen_ref[d, pl.ds(first, 1), :] for d in range(3)]
            + [jnp.zeros((4, BS), F32)],
            axis=0,
        )
        columns = jnp.transpose(params)
        decay = -columns[:, 0:1]
        row_x = jnp.exp(decay * (step_x * spacing - columns[:, 1:2]) ** 2)
        row_yz = jnp.exp(
            decay
            * (
                (step_y * spacing - columns[:, 2:3]) ** 2
                + (step_z * spacing - columns[:, 3:4]) ** 2
            )
        )
        block = block_ref[k]
        for n in range(EDGE):
            col_values = (col_x[n : n + 1] * col_yz).astype(BF16)
            product = lax.dot_general(block, col_values, NT, preferred_element_type=F32)
            weighted = product * row_yz * row_x[:, n : n + 1]
            dens_ref[pl.ds(k, 1), n * 256 : n * 256 + 256] = jnp.sum(
                weighted, axis=0, keepdims=True
            )
        place = (group & 7) * GROUP + tag
        number = (group >> 3) * OWN + (place & 1) * PLANE + (place >> 1)
        return jnp.where(rows((ITEMS, 128)) == k, number.astype(F32), targets)

    numbers = lax.fori_loop(0, ITEMS // 2, item, jnp.zeros((ITEMS, 128), F32))
    pl.semaphore_wait(barrier, NR + NC + NZ - 3)
    for n in range(1, NC):
        pl.semaphore_signal(again_sem, inc=1, device_id=(r, ys[n], z), device_id_type=MESH)
    numbers = lax.fori_loop(ITEMS // 2, ITEMS, item, numbers)

    lane = lanes((ITEMS, 128))
    extra = jnp.where(lane == TARGET, numbers, 0.0)
    for c, q in enumerate(CORNERS):
        tile = dens_ref[:, q // 128 * 128 : q // 128 * 128 + 128]
        extra = jnp.where(lane == CORNER + c, roll(tile, CORNER + c - q), extra)
    lower = lane < 64

    def beside(x):
        return pltpu.roll(roll(x, 64), 4, 0)

    extra = jnp.where(lower, extra, beside(extra))
    point = (lane & 63) < SUB
    for t in range(PTS // 128):
        tile = dens_ref[:, t * 128 : t * 128 + 128]
        other = beside(tile)
        for m in range(3):
            value = jnp.where(lower, roll(tile, -SUB * m), roll(other, -SUB * m))
            a_out[3 * t + m] = jnp.where(point, value, extra)[:4]
    pl.semaphore_wait(again_sem, NC - 1)

    def plane_copies(out, got, send, recv):
        for dy, dz in PLANE_STEPS:
            pltpu.make_async_remote_copy(
                src_ref=out.at[ys[dy] * NZ + zs[dz]],
                dst_ref=got.at[me],
                send_sem=send,
                recv_sem=recv,
                device_id=(r, ys[dy], zs[dz]),
                device_id_type=MESH,
            ).start()
        got[me] = out[me]

    def arrived(ref, count, sem):
        whole = ref.at[pl.ds(0, count)]
        pltpu.make_async_copy(whole, whole, sem).wait()

    plane_copies(a_out, a_got, a_send, a_recv)
    arrived(a_got, PLANE - 1, a_recv)

    turned = jnp.transpose(
        jnp.concatenate([a_got[a] for a in range(PLANE)], axis=0)
    )
    values = jnp.concatenate([turned[:ROWS], turned[64 : 64 + ROWS]], axis=1)
    high = values.astype(BF16)
    low = (values - high.astype(F32)).astype(BF16)
    left = jnp.concatenate([high, low], axis=0)
    wanted = values[TARGET : TARGET + 1, :]
    count = rows((128, PLANE * ITEMS)).astype(F32)
    count2 = jnp.where(count < 64.0, count + 128.0, count + 64.0)
    half = lanes((32, 128)) < 64

    def table(row):
        here = wanted - (row * OWN).astype(F32)
        parts = []
        for at in (count, count2):
            right = jnp.where(at == here, 1.0, 0.0).astype(BF16)
            both = lax.dot_general(left, right, NT, preferred_element_type=F32)
            parts.append(both[:ROWS] + both[ROWS:])
        whole, mixed = parts
        mixed = jnp.concatenate([mixed, jnp.zeros((64 - ROWS, 128), F32)], axis=0)
        return jnp.concatenate([whole, jnp.where(half, mixed[:32], mixed[32:])], axis=0)

    for n, other in enumerate(row_of):
        r_out[n] = table(other)
        pltpu.make_async_remote_copy(
            src_ref=r_out.at[n],
            dst_ref=r_got.at[n],
            send_sem=r_send,
            recv_sem=r_recv,
            device_id=(other, y, z),
            device_id_type=MESH,
        ).start()
    total = table(r)
    arrived(r_got, NR - 1, r_recv)
    for n in range(NR - 1):
        total = total + r_got[n]
    whole, mixed = total[:ROWS], total[ROWS:]
    mixed = jnp.concatenate([mixed, roll(mixed, 64)], axis=0)
    c_out[:, :128] = whole[CORNER : CORNER + 8]
    c_out[:, 128:] = mixed[CORNER : CORNER + 8]

    for other in row_of:
        pltpu.make_async_remote_copy(
            src_ref=c_out,
            dst_ref=c_got.at[r],
            send_sem=c_send,
            recv_sem=c_recv,
            device_id=(other, y, z),
            device_id_type=MESH,
        ).start()
    c_got[r] = c_out[...]

    whole = jnp.concatenate([whole, jnp.zeros((64 - ROWS, 128), F32)], axis=0)
    second = jnp.where(lanes((64, 128)) < 32, roll(whole, 32), roll(mixed, 32))
    bricks = jnp.transpose(jnp.concatenate([whole, second], axis=0))
    for a in range(PLANE):
        b_out[a] = bricks[a : a + 1]
    plane_copies(b_out, b_got, b_send, b_recv)

    arrived(c_got, NR - 1, c_recv)
    kept, added = [], []
    for b in range(2):
        means = []
        for h in range(2):
            ref = refs_ref[b, :, h * 128 : h * 128 + 128]
            corner, brick = ref & 7, ref >> 3
            source = ((brick >> 6) * 11) >> 5
            place = brick - source * OWN
            place = (place >> 1) + (place & 1) * PLANE
            at = place & 127
            which = (source * 2 + (place >> 7)) * 8 + corner
            found = jnp.zeros((8, 128), F32)
            for n in range(NR):
                for part in range(2):
                    for c in range(8):
                        line = jnp.broadcast_to(
                            c_got[n, c : c + 1, part * 128 : part * 128 + 128], (8, 128)
                        )
                        here = jnp.take_along_axis(line, at, axis=1)
                        found = jnp.where(which == (n * 2 + part) * 8 + c, here, found)
            means.append(jnp.sum(found, axis=0, keepdims=True) * 0.0625)
        mean = jnp.concatenate(means, axis=1)
        cell = cell_ref[b : b + 1, :]
        upper = rows((32, 256)) == (cell >> 7)
        coarse = mean.astype(BF16).astype(F32)
        weights = jnp.concatenate(
            [
                jnp.where(upper, coarse, 0.0),
                jnp.where(upper, mean - coarse, 0.0),
                jnp.where(upper, 0.5, 0.0),
            ],
            axis=0,
        ).astype(BF16)
        spots = jnp.where(rows((128, 256)) == (cell & 127), 1.0, 0.0).astype(BF16)
        spread = lax.dot_general(weights, spots, NT, preferred_element_type=F32)
        added.append(spread[:32] + spread[32:64])
        kept.append(1.0 - spread[64:])

    arrived(b_got, PLANE - 1, b_recv)
    lane = lanes((1, 128))
    for b in range(2):
        for t in range(PTS // 128):
            thirds = [roll(b_got[3 * t + m], SUB * m - 64 * b) for m in range(3)]
            value = jnp.where(
                lane < SUB, thirds[0], jnp.where(lane < 2 * SUB, thirds[1], thirds[2])
            )
            out_ref[b : b + 1, t * 128 : t * 128 + 128] = (
                value * kept[b][t : t + 1] + added[b][t : t + 1]
            )
    arrived(a_out, PLANE - 1, a_send)
    arrived(r_out, NR - 1, r_send)
    arrived(b_out, PLANE - 1, b_send)
    arrived(c_got, NR - 1, c_send)


def body(
    block_data, item_pairs, dest_slot, brick_tag, centres, exponents, levels, cell_pos, corner_refs
):
    arguments = (
        item_pairs.T,
        dest_slot,
        brick_tag,
        levels,
        centres.transpose(1, 0, 2),
        exponents,
        block_data,
        corner_refs.transpose(0, 2, 1),
        cell_pos,
    )
    places = [pltpu.SMEM] * 4 + [pltpu.VMEM] * 5
    dma = pltpu.SemaphoreType.DMA
    return pl.pallas_call(
        kernel,
        out_shape=pltpu.VMEM((2, PTS), F32),
        in_specs=[pl.BlockSpec(memory_space=pltpu.HBM)] * len(arguments),
        out_specs=pl.BlockSpec(memory_space=pltpu.VMEM),
        scratch_shapes=[place(a.shape, a.dtype) for place, a in zip(places, arguments)]
        + [
            pltpu.VMEM((ITEMS, PTS), F32),
            pltpu.VMEM((PLANE, 4, 128), F32),
            pltpu.VMEM((PLANE, 4, 128), F32),
            pltpu.VMEM((NR - 1, ROWS + 32, 128), F32),
            pltpu.VMEM((NR - 1, ROWS + 32, 128), F32),
            pltpu.VMEM((PLANE, 1, 128), F32),
            pltpu.VMEM((PLANE, 1, 128), F32),
            pltpu.VMEM((8, 256), F32),
            pltpu.VMEM((NR, 8, 256), F32),
            dma((len(arguments),)),
            pltpu.SemaphoreType.REGULAR,
        ]
        + [dma] * 8,
        compiler_params=pltpu.CompilerParams(
            collective_id=0, has_side_effects=True, vmem_limit_bytes=60 * 2**20
        ),
        name="collocate",
    )(*arguments)


def solution(mesh):
    spread = ("row", "col", "basis")
    return jax.shard_map(
        body,
        mesh=mesh,
        in_specs=(
            P(spread, None, None),
            P(spread, None),
            P(spread),
            P(spread),
            P(),
            P(),
            P(),
            P(spread, None),
            P(spread, None, None),
        ),
        out_specs=P(spread, None),
        check_vma=False,
    )
```

```python
import itertools

import jax
import jax.numpy as jnp
from jax import lax
from jax.experimental import pallas as pl
from jax.experimental.pallas import tpu as pltpu
from jax.sharding import PartitionSpec as P

MESH = pl.DeviceIdType.MESH
F32 = jnp.float32
BF16 = jnp.bfloat16

EDGE = 16
HALF = (EDGE - 1) / 2.0
PTS = EDGE**3
BS = 128
ITEMS = 8
NR, NC, NZ = 8, 8, 12
PLANE = NC * NZ
GROUP = 24
OWN = NC * GROUP
SUB = 43
TARGET = SUB
CORNER = 48
ROWS = 56
NT = (((1,), (1,)), ((), ()))
CORNERS = tuple(
    ((c // 4) * 15 * EDGE + (c // 2 % 2) * 15) * EDGE + (c % 2) * 15 for c in range(8)
)


def far(step, size):
    return min(step, size - step)


PLANE_STEPS = sorted(
    (s for s in itertools.product(range(NC), range(NZ)) if any(s)),
    key=lambda s: -(far(s[0], NC) + far(s[1], NZ)),
)
ROW_STEPS = ((2, 1), (2, 0), (1, 1), (3, 1), (1, 0), (3, 0), (0, 1))


def lanes(shape):
    return lax.broadcasted_iota(jnp.int32, shape, len(shape) - 1)


def rows(shape):
    return lax.broadcasted_iota(jnp.int32, shape, len(shape) - 2)


def roll(x, shift):
    shift %= x.shape[-1]
    return x if shift == 0 else pltpu.roll(x, shift, x.ndim - 1)


def kernel(
    pairs_hbm,
    slot_hbm,
    tag_hbm,
    levels_hbm,
    cen_hbm,
    exp_hbm,
    block_hbm,
    refs_hbm,
    cell_hbm,
    out_ref,
    pairs_ref,
    slot_ref,
    tag_ref,
    levels_ref,
    cen_ref,
    exp_ref,
    block_ref,
    refs_ref,
    cell_ref,
    colx_ref,
    colyz_ref,
    rowx_ref,
    rowyz_ref,
    dens_ref,
    a_out,
    a_got,
    r_out,
    r_got,
    b_out,
    b_got,
    c_out,
    c_got,
    load_sem,
    again_sem,
    a_send,
    a_recv,
    r_send,
    r_recv,
    b_send,
    b_recv,
    c_send,
    c_recv,
):
    loads = [
        pltpu.make_async_copy(source, into, load_sem.at[n])
        for n, (source, into) in enumerate(
            (
                (pairs_hbm, pairs_ref),
                (slot_hbm, slot_ref),
                (tag_hbm, tag_ref),
                (levels_hbm, levels_ref),
                (cen_hbm, cen_ref),
                (exp_hbm, exp_ref),
                (block_hbm, block_ref),
                (refs_hbm, refs_ref),
                (cell_hbm, cell_ref),
            )
        )
    ]
    r, y, z = (lax.axis_index(a) for a in ("row", "col", "basis"))
    ys = [lax.rem(y + n, NC) for n in range(NC)]
    zs = [lax.rem(z + n, NZ) for n in range(NZ)]
    x, core = r // 2, lax.rem(r, 2)
    xs = [lax.rem(x + n, NR // 2) * 2 for n in range(NR // 2)]
    cores = [core, 1 - core]
    row_of = [xs[dx] + cores[dc] for dx, dc in ROW_STEPS]
    me = y * NZ + z

    barrier = pltpu.get_barrier_semaphore()

    def entered(*device):
        pl.semaphore_signal(barrier, inc=1, device_id=device, device_id_type=MESH)

    col_steps = sorted(range(1, NC), key=lambda n: -far(n, NC))
    for n in col_steps:
        entered(r, ys[n], z)
    for load in loads:
        load.start()
    for n in sorted(range(1, NZ), key=lambda n: -far(n, NZ)):
        entered(r, y, zs[n])
    for other in row_of:
        entered(other, y, z)

    step16 = rows((EDGE, BS)).astype(F32) - HALF
    lane256 = lanes((1, EDGE * EDGE))
    step_y = (lane256 // EDGE).astype(F32) - HALF
    step_z = (lane256 % EDGE).astype(F32) - HALF
    lane = lanes((ITEMS, 128))
    for load in loads:
        load.wait()

    numbers = jnp.zeros((ITEMS, 128), F32)
    spacings, params, row_xs = [], [], []
    for k in range(ITEMS):
        first, second = pairs_ref[0, k], pairs_ref[1, k]
        group, tag = slot_ref[k], tag_ref[k]
        spacing = jnp.where(levels_ref[group * GROUP + tag] == 0, 0.2, 0.1).astype(F32)
        spacings.append(spacing)
        place = (group & 7) * GROUP + tag
        number = (group >> 3) * OWN + (place & 1) * PLANE + (place >> 1)
        numbers = jnp.where(rows((ITEMS, 128)) == k, number.astype(F32), numbers)

        points = step16 * spacing
        rate = exp_ref[pl.ds(second, 1), :]
        middle = [cen_ref[d, pl.ds(second, 1), :] for d in range(3)]
        col_x, col_y, col_z = [jnp.exp(-rate * (points - m) ** 2) for m in middle]
        colx_ref[k] = col_x
        for n in range(EDGE):
            colyz_ref[k, n * EDGE : n * EDGE + EDGE, :] = col_y[n : n + 1] * col_z

        rate = exp_ref[pl.ds(first, 1), :]
        middle = [cen_ref[d, pl.ds(first, 1), :] for d in range(3)]
        row_xs.append(jnp.exp(-rate * (points - middle[0]) ** 2))
        params += [-rate, middle[1], middle[2]]
    columns = jnp.transpose(
        jnp.concatenate(params + [jnp.zeros((32 - 3 * ITEMS, BS), F32)], axis=0)
    )
    row_x = jnp.transpose(jnp.concatenate(row_xs, axis=0))
    for k in range(ITEMS):
        rowx_ref[k] = roll(row_x, -EDGE * k)
        decay, middle_y, middle_z = (columns[:, 3 * k + n : 3 * k + n + 1] for n in range(3))
        rowyz_ref[k] = jnp.exp(
            decay
            * (
                (step_y * spacings[k] - middle_y) ** 2
                + (step_z * spacings[k] - middle_z) ** 2
            )
        )

    def item(k, carry):
        block = block_ref[k]
        col_x = colx_ref[k]
        row_x = rowx_ref[k]
        for n in range(EDGE):
            col_values = (col_x[n : n + 1] * colyz_ref[k]).astype(BF16)
            product = lax.dot_general(block, col_values, NT, preferred_element_type=F32)
            weighted = product * rowyz_ref[k] * row_x[:, n : n + 1]
            dens_ref[pl.ds(k, 1), n * 256 : n * 256 + 256] = jnp.sum(
                weighted, axis=0, keepdims=True
            )
        return carry

    lax.fori_loop(0, ITEMS // 2, item, 0, unroll=True)
    pl.semaphore_wait(barrier, NR + NC + NZ - 3)
    for n in col_steps:
        pl.semaphore_signal(again_sem, inc=1, device_id=(r, ys[n], z), device_id_type=MESH)
    lax.fori_loop(ITEMS // 2, ITEMS, item, 0, unroll=True)

    extra = jnp.where(lane == TARGET, numbers, 0.0)
    for c, q in enumerate(CORNERS):
        tile = dens_ref[:, q // 128 * 128 : q // 128 * 128 + 128]
        extra = jnp.where(lane == CORNER + c, roll(tile, CORNER + c - q), extra)
    lower = lane < 64

    def beside(x):
        return pltpu.roll(roll(x, 64), 4, 0)

    extra = jnp.where(lower, extra, beside(extra))
    point = (lane & 63) < SUB
    for t in range(PTS // 128):
        tile = dens_ref[:, t * 128 : t * 128 + 128]
        other = beside(tile)
        for m in range(3):
            value = jnp.where(lower, roll(tile, -SUB * m), roll(other, -SUB * m))
            a_out[3 * t + m] = jnp.where(point, value, extra)[:4]
    pl.semaphore_wait(again_sem, NC - 1)

    def plane_copies(out, got, send, recv):
        for dy, dz in PLANE_STEPS:
            pltpu.make_async_remote_copy(
                src_ref=out.at[ys[dy] * NZ + zs[dz]],
                dst_ref=got.at[me],
                send_sem=send,
                recv_sem=recv,
                device_id=(r, ys[dy], zs[dz]),
                device_id_type=MESH,
            ).start()
        got[me] = out[me]

    def arrived(ref, count, sem):
        whole = ref.at[pl.ds(0, count)]
        pltpu.make_async_copy(whole, whole, sem).wait()

    plane_copies(a_out, a_got, a_send, a_recv)
    arrived(a_got, PLANE - 1, a_recv)

    turned = jnp.transpose(
        jnp.concatenate([a_got[a] for a in range(PLANE)], axis=0)
    )
    values = jnp.concatenate([turned[:ROWS], turned[64 : 64 + ROWS]], axis=1)
    high = values.astype(BF16)
    low = (values - high.astype(F32)).astype(BF16)
    left = jnp.concatenate([high, low], axis=0)
    wanted = values[TARGET : TARGET + 1, :]
    count = rows((128, PLANE * ITEMS)).astype(F32)
    count2 = jnp.where(count < 64.0, count + 128.0, count + 64.0)
    half = lanes((32, 128)) < 64

    def table(row):
        here = wanted - (row * OWN).astype(F32)
        parts = []
        for at in (count, count2):
            right = jnp.where(at == here, 1.0, 0.0).astype(BF16)
            both = lax.dot_general(left, right, NT, preferred_element_type=F32)
            parts.append(both[:ROWS] + both[ROWS:])
        whole, mixed = parts
        mixed = jnp.concatenate([mixed, jnp.zeros((64 - ROWS, 128), F32)], axis=0)
        return jnp.concatenate([whole, jnp.where(half, mixed[:32], mixed[32:])], axis=0)

    for n, other in enumerate(row_of):
        r_out[n] = table(other)
        pltpu.make_async_remote_copy(
            src_ref=r_out.at[n],
            dst_ref=r_got.at[n],
            send_sem=r_send,
            recv_sem=r_recv,
            device_id=(other, y, z),
            device_id_type=MESH,
        ).start()
    total = table(r)
    arrived(r_got, NR - 1, r_recv)
    for n in range(NR - 1):
        total = total + r_got[n]
    whole, mixed = total[:ROWS], total[ROWS:]
    mixed = jnp.concatenate([mixed, roll(mixed, 64)], axis=0)
    c_out[:, :128] = whole[CORNER : CORNER + 8]
    c_out[:, 128:] = mixed[CORNER : CORNER + 8]

    for other in row_of:
        pltpu.make_async_remote_copy(
            src_ref=c_out,
            dst_ref=c_got.at[r],
            send_sem=c_send,
            recv_sem=c_recv,
            device_id=(other, y, z),
            device_id_type=MESH,
        ).start()
    c_got[r] = c_out[...]

    whole = jnp.concatenate([whole, jnp.zeros((64 - ROWS, 128), F32)], axis=0)
    second = jnp.where(lanes((64, 128)) < 32, roll(whole, 32), roll(mixed, 32))
    bricks = jnp.transpose(jnp.concatenate([whole, second], axis=0))
    for a in range(PLANE):
        b_out[a] = bricks[a : a + 1]
    plane_copies(b_out, b_got, b_send, b_recv)

    arrived(c_got, NR - 1, c_recv)
    kept, added = [], []
    for b in range(2):
        means = []
        for h in range(2):
            ref = refs_ref[b, :, h * 128 : h * 128 + 128]
            corner, brick = ref & 7, ref >> 3
            source = ((brick >> 6) * 11) >> 5
            place = brick - source * OWN
            place = (place >> 1) + (place & 1) * PLANE
            at = place & 127
            which = (source * 2 + (place >> 7)) * 8 + corner
            found = jnp.zeros((8, 128), F32)
            for n in range(NR):
                for part in range(2):
                    for c in range(8):
                        line = jnp.broadcast_to(
                            c_got[n, c : c + 1, part * 128 : part * 128 + 128], (8, 128)
                        )
                        here = jnp.take_along_axis(line, at, axis=1)
                        found = jnp.where(which == (n * 2 + part) * 8 + c, here, found)
            means.append(jnp.sum(found, axis=0, keepdims=True) * 0.0625)
        mean = jnp.concatenate(means, axis=1)
        cell = cell_ref[b : b + 1, :]
        upper = rows((32, 256)) == (cell >> 7)
        coarse = mean.astype(BF16).astype(F32)
        weights = jnp.concatenate(
            [
                jnp.where(upper, coarse, 0.0),
                jnp.where(upper, mean - coarse, 0.0),
                jnp.where(upper, 0.5, 0.0),
            ],
            axis=0,
        ).astype(BF16)
        spots = jnp.where(rows((128, 256)) == (cell & 127), 1.0, 0.0).astype(BF16)
        spread = lax.dot_general(weights, spots, NT, preferred_element_type=F32)
        added.append(spread[:32] + spread[32:64])
        kept.append(1.0 - spread[64:])

    arrived(b_got, PLANE - 1, b_recv)
    lane = lanes((1, 128))
    for b in range(2):
        for t in range(PTS // 128):
            thirds = [roll(b_got[3 * t + m], SUB * m - 64 * b) for m in range(3)]
            value = jnp.where(
                lane < SUB, thirds[0], jnp.where(lane < 2 * SUB, thirds[1], thirds[2])
            )
            out_ref[b : b + 1, t * 128 : t * 128 + 128] = (
                value * kept[b][t : t + 1] + added[b][t : t + 1]
            )
    arrived(a_out, PLANE - 1, a_send)
    arrived(r_out, NR - 1, r_send)
    arrived(b_out, PLANE - 1, b_send)
    arrived(c_got, NR - 1, c_send)


def body(
    block_data, item_pairs, dest_slot, brick_tag, centres, exponents, levels, cell_pos, corner_refs
):
    arguments = (
        item_pairs.T,
        dest_slot,
        brick_tag,
        levels,
        centres.transpose(1, 0, 2),
        exponents,
        block_data,
        corner_refs.transpose(0, 2, 1),
        cell_pos,
    )
    places = [pltpu.SMEM] * 4 + [pltpu.VMEM] * 5
    dma = pltpu.SemaphoreType.DMA
    return pl.pallas_call(
        kernel,
        out_shape=pltpu.VMEM((2, PTS), F32),
        in_specs=[pl.BlockSpec(memory_space=pltpu.HBM)] * len(arguments),
        out_specs=pl.BlockSpec(memory_space=pltpu.VMEM),
        scratch_shapes=[place(a.shape, a.dtype) for place, a in zip(places, arguments)]
        + [
            pltpu.VMEM((ITEMS, EDGE, BS), F32),
            pltpu.VMEM((ITEMS, EDGE * EDGE, BS), F32),
            pltpu.VMEM((ITEMS, BS, 128), F32),
            pltpu.VMEM((ITEMS, BS, EDGE * EDGE), F32),
            pltpu.VMEM((ITEMS, PTS), F32),
            pltpu.VMEM((PLANE, 4, 128), F32),
            pltpu.VMEM((PLANE, 4, 128), F32),
            pltpu.VMEM((NR - 1, ROWS + 32, 128), F32),
            pltpu.VMEM((NR - 1, ROWS + 32, 128), F32),
            pltpu.VMEM((PLANE, 1, 128), F32),
            pltpu.VMEM((PLANE, 1, 128), F32),
            pltpu.VMEM((8, 256), F32),
            pltpu.VMEM((NR, 8, 256), F32),
            dma((len(arguments),)),
            pltpu.SemaphoreType.REGULAR,
        ]
        + [dma] * 8,
        compiler_params=pltpu.CompilerParams(
            collective_id=0, has_side_effects=True, vmem_limit_bytes=60 * 2**20
        ),
        name="collocate",
    )(*arguments)


def solution(mesh):
    spread = ("row", "col", "basis")
    return jax.shard_map(
        body,
        mesh=mesh,
        in_specs=(
            P(spread, None, None),
            P(spread, None),
            P(spread),
            P(spread),
            P(),
            P(),
            P(),
            P(spread, None),
            P(spread, None, None),
        ),
        out_specs=P(spread, None),
        check_vma=False,
    )
```

```python
import itertools

import jax
import jax.numpy as jnp
from jax import lax
from jax.experimental import pallas as pl
from jax.experimental.pallas import tpu as pltpu
from jax.sharding import PartitionSpec as P

MESH = pl.DeviceIdType.MESH
F32 = jnp.float32
BF16 = jnp.bfloat16

EDGE = 16
HALF = (EDGE - 1) / 2.0
PTS = EDGE**3
BS = 128
ITEMS = 8
NR, NC, NZ = 8, 8, 12
NX = NR // 2
PLANE = NC * NZ
GROUP = 24
OWN = NC * GROUP
SUB = 43
TARGET = SUB
CORNER = 48
ROWS = 56
NT = (((1,), (1,)), ((), ()))
CORNERS = tuple(
    ((c // 4) * 15 * EDGE + (c // 2 % 2) * 15) * EDGE + (c % 2) * 15 for c in range(8)
)


def far(step, size):
    return min(step, size - step)


PLANE_STEPS = sorted(
    (s for s in itertools.product(range(NC), range(NZ)) if any(s)),
    key=lambda s: -(far(s[0], NC) + far(s[1], NZ)),
)
CHIP_STEPS = (2, 1, 3, 0)
ROW_STEPS = ((2, 1), (2, 0), (1, 1), (3, 1), (1, 0), (3, 0), (0, 1))


def lanes(shape):
    return lax.broadcasted_iota(jnp.int32, shape, len(shape) - 1)


def rows(shape):
    return lax.broadcasted_iota(jnp.int32, shape, len(shape) - 2)


def roll(x, shift):
    shift %= x.shape[-1]
    return x if shift == 0 else pltpu.roll(x, shift, x.ndim - 1)


def kernel(
    pairs_hbm,
    slot_hbm,
    tag_hbm,
    levels_hbm,
    cen_hbm,
    exp_hbm,
    block_hbm,
    refs_hbm,
    cell_hbm,
    out_ref,
    pairs_ref,
    slot_ref,
    tag_ref,
    levels_ref,
    cen_ref,
    exp_ref,
    block_ref,
    refs_ref,
    cell_ref,
    colx_ref,
    colyz_ref,
    rowx_ref,
    rowyz_ref,
    dens_ref,
    a_out,
    a_got,
    h_out,
    h_got,
    r_out,
    r_got,
    b_out,
    b_got,
    c_out,
    c_got,
    load_sem,
    again_sem,
    a_send,
    a_recv,
    h_send,
    h_recv,
    r_send,
    r_recv,
    b_send,
    b_recv,
    c_send,
    c_recv,
):
    loads = [
        pltpu.make_async_copy(source, into, load_sem.at[n])
        for n, (source, into) in enumerate(
            (
                (pairs_hbm, pairs_ref),
                (slot_hbm, slot_ref),
                (tag_hbm, tag_ref),
                (levels_hbm, levels_ref),
                (cen_hbm, cen_ref),
                (exp_hbm, exp_ref),
                (block_hbm, block_ref),
                (refs_hbm, refs_ref),
                (cell_hbm, cell_ref),
            )
        )
    ]
    r, y, z = (lax.axis_index(a) for a in ("row", "col", "basis"))
    ys = [lax.rem(y + n, NC) for n in range(NC)]
    zs = [lax.rem(z + n, NZ) for n in range(NZ)]
    x, core = r // 2, lax.rem(r, 2)
    xs = [lax.rem(x + n, NX) * 2 for n in range(NX)]
    cores = [core, 1 - core]
    row_of = [xs[dx] + cores[dc] for dx, dc in ROW_STEPS]
    me = y * NZ + z

    barrier = pltpu.get_barrier_semaphore()

    def entered(*device):
        pl.semaphore_signal(barrier, inc=1, device_id=device, device_id_type=MESH)

    col_steps = sorted(range(1, NC), key=lambda n: -far(n, NC))
    for n in col_steps:
        entered(r, ys[n], z)
    for load in loads:
        load.start()
    for n in sorted(range(1, NZ), key=lambda n: -far(n, NZ)):
        entered(r, y, zs[n])
    for other in row_of:
        entered(other, y, z)

    step16 = rows((EDGE, BS)).astype(F32) - HALF
    lane256 = lanes((1, EDGE * EDGE))
    step_y = (lane256 // EDGE).astype(F32) - HALF
    step_z = (lane256 % EDGE).astype(F32) - HALF
    lane = lanes((ITEMS, 128))
    for load in loads:
        load.wait()

    numbers = jnp.zeros((ITEMS, 128), F32)
    spacings, params, row_xs = [], [], []
    for k in range(ITEMS):
        first, second = pairs_ref[0, k], pairs_ref[1, k]
        group, tag = slot_ref[k], tag_ref[k]
        spacing = jnp.where(levels_ref[group * GROUP + tag] == 0, 0.2, 0.1).astype(F32)
        spacings.append(spacing)
        place = (group & 7) * GROUP + tag
        number = (group >> 3) * OWN + (place & 1) * PLANE + (place >> 1)
        numbers = jnp.where(rows((ITEMS, 128)) == k, number.astype(F32), numbers)

        points = step16 * spacing
        rate = exp_ref[pl.ds(second, 1), :]
        middle = [cen_ref[d, pl.ds(second, 1), :] for d in range(3)]
        col_x, col_y, col_z = [jnp.exp(-rate * (points - m) ** 2) for m in middle]
        colx_ref[k] = col_x
        for n in range(EDGE):
            colyz_ref[k, n * EDGE : n * EDGE + EDGE, :] = col_y[n : n + 1] * col_z

        rate = exp_ref[pl.ds(first, 1), :]
        middle = [cen_ref[d, pl.ds(first, 1), :] for d in range(3)]
        row_xs.append(jnp.exp(-rate * (points - middle[0]) ** 2))
        params += [-rate, middle[1], middle[2]]
    columns = jnp.transpose(
        jnp.concatenate(params + [jnp.zeros((32 - 3 * ITEMS, BS), F32)], axis=0)
    )
    row_x = jnp.transpose(jnp.concatenate(row_xs, axis=0))
    for k in range(ITEMS):
        rowx_ref[k] = roll(row_x, -EDGE * k)
        decay, middle_y, middle_z = (columns[:, 3 * k + n : 3 * k + n + 1] for n in range(3))
        rowyz_ref[k] = jnp.exp(
            decay
            * (
                (step_y * spacings[k] - middle_y) ** 2
                + (step_z * spacings[k] - middle_z) ** 2
            )
        )

    def item(k, carry):
        block = block_ref[k]
        col_x = colx_ref[k]
        row_x = rowx_ref[k]
        for n in range(EDGE):
            col_values = (col_x[n : n + 1] * colyz_ref[k]).astype(BF16)
            product = lax.dot_general(block, col_values, NT, preferred_element_type=F32)
            weighted = product * rowyz_ref[k] * row_x[:, n : n + 1]
            dens_ref[pl.ds(k, 1), n * 256 : n * 256 + 256] = jnp.sum(
                weighted, axis=0, keepdims=True
            )
        return carry

    lax.fori_loop(0, ITEMS // 2, item, 0, unroll=True)
    pl.semaphore_wait(barrier, NR + NC + NZ - 3)
    for n in col_steps:
        pl.semaphore_signal(again_sem, inc=1, device_id=(r, ys[n], z), device_id_type=MESH)
    lax.fori_loop(ITEMS // 2, ITEMS, item, 0, unroll=True)

    extra = jnp.where(lane == TARGET, numbers, 0.0)
    for c, q in enumerate(CORNERS):
        tile = dens_ref[:, q // 128 * 128 : q // 128 * 128 + 128]
        extra = jnp.where(lane == CORNER + c, roll(tile, CORNER + c - q), extra)
    lower = lane < 64

    def beside(x):
        return pltpu.roll(roll(x, 64), 4, 0)

    extra = jnp.where(lower, extra, beside(extra))
    point = (lane & 63) < SUB
    for t in range(PTS // 128):
        tile = dens_ref[:, t * 128 : t * 128 + 128]
        other = beside(tile)
        for m in range(3):
            value = jnp.where(lower, roll(tile, -SUB * m), roll(other, -SUB * m))
            a_out[3 * t + m] = jnp.where(point, value, extra)[:4]
    pl.semaphore_wait(again_sem, NC - 1)

    def plane_copies(out, got, send, recv):
        for dy, dz in PLANE_STEPS:
            pltpu.make_async_remote_copy(
                src_ref=out.at[ys[dy] * NZ + zs[dz]],
                dst_ref=got.at[me],
                send_sem=send,
                recv_sem=recv,
                device_id=(r, ys[dy], zs[dz]),
                device_id_type=MESH,
            ).start()
        got[me] = out[me]

    def arrived(ref, count, sem):
        whole = ref.at[pl.ds(0, count)]
        pltpu.make_async_copy(whole, whole, sem).wait()

    plane_copies(a_out, a_got, a_send, a_recv)
    arrived(a_got, PLANE - 1, a_recv)

    turned = jnp.transpose(
        jnp.concatenate([a_got[a] for a in range(PLANE)], axis=0)
    )
    values = jnp.concatenate([turned[:ROWS], turned[64 : 64 + ROWS]], axis=1)
    high = values.astype(BF16)
    low = (values - high.astype(F32)).astype(BF16)
    left = jnp.concatenate([high, low], axis=0)
    wanted = values[TARGET : TARGET + 1, :]
    count = rows((128, PLANE * ITEMS)).astype(F32)
    count2 = jnp.where(count < 64.0, count + 128.0, count + 64.0)
    half = lanes((32, 128)) < 64

    def table(row):
        here = wanted - (row * OWN).astype(F32)
        parts = []
        for at in (count, count2):
            right = jnp.where(at == here, 1.0, 0.0).astype(BF16)
            both = lax.dot_general(left, right, NT, preferred_element_type=F32)
            parts.append(both[:ROWS] + both[ROWS:])
        whole, mixed = parts
        mixed = jnp.concatenate([mixed, jnp.zeros((64 - ROWS, 128), F32)], axis=0)
        return jnp.concatenate([whole, jnp.where(half, mixed[:32], mixed[32:])], axis=0)

    halves = []
    for n, dx in enumerate(CHIP_STEPS):
        h_out[n] = table(xs[dx] + cores[1])
        half_copy = pltpu.make_async_remote_copy(
            src_ref=h_out.at[n],
            dst_ref=h_got.at[n],
            send_sem=h_send,
            recv_sem=h_recv.at[n],
            device_id=(xs[0] + cores[1], y, z),
            device_id_type=MESH,
        )
        half_copy.start()
        halves.append(half_copy)
    for n, dx in enumerate(CHIP_STEPS):
        r_out[n] = table(xs[dx] + core)
    for n, dx in enumerate(CHIP_STEPS[:-1]):
        halves[n].wait_recv()
        r_out[n] = r_out[n] + h_got[n]
        pltpu.make_async_remote_copy(
            src_ref=r_out.at[n],
            dst_ref=r_got.at[n],
            send_sem=r_send,
            recv_sem=r_recv,
            device_id=(xs[dx] + core, y, z),
            device_id_type=MESH,
        ).start()
    halves[-1].wait_recv()
    total = r_out[NX - 1] + h_got[NX - 1]
    arrived(r_got, NX - 1, r_recv)
    for n in range(NX - 1):
        total = total + r_got[n]
    whole, mixed = total[:ROWS], total[ROWS:]
    mixed = jnp.concatenate([mixed, roll(mixed, 64)], axis=0)

    whole = jnp.concatenate([whole, jnp.zeros((64 - ROWS, 128), F32)], axis=0)
    second = jnp.where(lanes((64, 128)) < 32, roll(whole, 32), roll(mixed, 32))
    bricks = jnp.transpose(jnp.concatenate([whole, second], axis=0))
    for a in range(PLANE):
        b_out[a] = bricks[a : a + 1]
    plane_copies(b_out, b_got, b_send, b_recv)

    c_out[:, :128] = whole[CORNER : CORNER + 8]
    c_out[:, 128:] = mixed[CORNER : CORNER + 8]
    for other in row_of:
        pltpu.make_async_remote_copy(
            src_ref=c_out,
            dst_ref=c_got.at[r],
            send_sem=c_send,
            recv_sem=c_recv,
            device_id=(other, y, z),
            device_id_type=MESH,
        ).start()
    c_got[r] = c_out[...]

    arrived(c_got, NR - 1, c_recv)
    kept, added = [], []
    for b in range(2):
        means = []
        for h in range(2):
            ref = refs_ref[b, :, h * 128 : h * 128 + 128]
            corner, brick = ref & 7, ref >> 3
            source = ((brick >> 6) * 11) >> 5
            place = brick - source * OWN
            place = (place >> 1) + (place & 1) * PLANE
            at = place & 127
            which = (source * 2 + (place >> 7)) * 8 + corner
            found = jnp.zeros((8, 128), F32)
            for n in range(NR):
                for part in range(2):
                    for c in range(8):
                        line = jnp.broadcast_to(
                            c_got[n, c : c + 1, part * 128 : part * 128 + 128], (8, 128)
                        )
                        here = jnp.take_along_axis(line, at, axis=1)
                        found = jnp.where(which == (n * 2 + part) * 8 + c, here, found)
            means.append(jnp.sum(found, axis=0, keepdims=True) * 0.0625)
        mean = jnp.concatenate(means, axis=1)
        cell = cell_ref[b : b + 1, :]
        upper = rows((32, 256)) == (cell >> 7)
        coarse = mean.astype(BF16).astype(F32)
        weights = jnp.concatenate(
            [
                jnp.where(upper, coarse, 0.0),
                jnp.where(upper, mean - coarse, 0.0),
                jnp.where(upper, 0.5, 0.0),
            ],
            axis=0,
        ).astype(BF16)
        spots = jnp.where(rows((128, 256)) == (cell & 127), 1.0, 0.0).astype(BF16)
        spread = lax.dot_general(weights, spots, NT, preferred_element_type=F32)
        added.append(spread[:32] + spread[32:64])
        kept.append(1.0 - spread[64:])

    arrived(b_got, PLANE - 1, b_recv)
    lane = lanes((1, 128))
    for b in range(2):
        for t in range(PTS // 128):
            thirds = [roll(b_got[3 * t + m], SUB * m - 64 * b) for m in range(3)]
            value = jnp.where(
                lane < SUB, thirds[0], jnp.where(lane < 2 * SUB, thirds[1], thirds[2])
            )
            out_ref[b : b + 1, t * 128 : t * 128 + 128] = (
                value * kept[b][t : t + 1] + added[b][t : t + 1]
            )
    arrived(a_out, PLANE - 1, a_send)
    arrived(h_out, NX, h_send)
    arrived(r_out, NX - 1, r_send)
    arrived(b_out, PLANE - 1, b_send)
    arrived(c_got, NR - 1, c_send)


def body(
    block_data, item_pairs, dest_slot, brick_tag, centres, exponents, levels, cell_pos, corner_refs
):
    arguments = (
        item_pairs.T,
        dest_slot,
        brick_tag,
        levels,
        centres.transpose(1, 0, 2),
        exponents,
        block_data,
        corner_refs.transpose(0, 2, 1),
        cell_pos,
    )
    places = [pltpu.SMEM] * 4 + [pltpu.VMEM] * 5
    dma = pltpu.SemaphoreType.DMA
    return pl.pallas_call(
        kernel,
        out_shape=pltpu.VMEM((2, PTS), F32),
        in_specs=[pl.BlockSpec(memory_space=pltpu.HBM)] * len(arguments),
        out_specs=pl.BlockSpec(memory_space=pltpu.VMEM),
        scratch_shapes=[place(a.shape, a.dtype) for place, a in zip(places, arguments)]
        + [
            pltpu.VMEM((ITEMS, EDGE, BS), F32),
            pltpu.VMEM((ITEMS, EDGE * EDGE, BS), F32),
            pltpu.VMEM((ITEMS, BS, 128), F32),
            pltpu.VMEM((ITEMS, BS, EDGE * EDGE), F32),
            pltpu.VMEM((ITEMS, PTS), F32),
            pltpu.VMEM((PLANE, 4, 128), F32),
            pltpu.VMEM((PLANE, 4, 128), F32),
            pltpu.VMEM((NX, ROWS + 32, 128), F32),
            pltpu.VMEM((NX, ROWS + 32, 128), F32),
            pltpu.VMEM((NX, ROWS + 32, 128), F32),
            pltpu.VMEM((NX - 1, ROWS + 32, 128), F32),
            pltpu.VMEM((PLANE, 1, 128), F32),
            pltpu.VMEM((PLANE, 1, 128), F32),
            pltpu.VMEM((8, 256), F32),
            pltpu.VMEM((NR, 8, 256), F32),
            dma((len(arguments),)),
            pltpu.SemaphoreType.REGULAR,
        ]
        + [dma, dma, dma, dma((NX,))]
        + [dma] * 6,
        compiler_params=pltpu.CompilerParams(
            collective_id=0, has_side_effects=True, vmem_limit_bytes=60 * 2**20
        ),
        name="collocate",
    )(*arguments)


def solution(mesh):
    spread = ("row", "col", "basis")
    return jax.shard_map(
        body,
        mesh=mesh,
        in_specs=(
            P(spread, None, None),
            P(spread, None),
            P(spread),
            P(spread),
            P(),
            P(),
            P(),
            P(spread, None),
            P(spread, None, None),
        ),
        out_specs=P(spread, None),
        check_vma=False,
    )
```

```python
import itertools

import jax
import jax.numpy as jnp
from jax import lax
from jax.experimental import pallas as pl
from jax.experimental.pallas import tpu as pltpu
from jax.sharding import PartitionSpec as P

MESH = pl.DeviceIdType.MESH
F32 = jnp.float32
BF16 = jnp.bfloat16

EDGE = 16
HALF = (EDGE - 1) / 2.0
PTS = EDGE**3
BS = 128
ITEMS = 8
NR, NC, NZ = 8, 8, 12
NX = NR // 2
PLANE = NC * NZ
GROUP = 24
OWN = NC * GROUP
SUB = 43
TARGET = SUB
CORNER = 48
ROWS = 56
NT = (((1,), (1,)), ((), ()))
CORNERS = tuple(
    ((c // 4) * 15 * EDGE + (c // 2 % 2) * 15) * EDGE + (c % 2) * 15 for c in range(8)
)


def far(step, size):
    return min(step, size - step)


PLANE_STEPS = sorted(
    (s for s in itertools.product(range(NC), range(NZ)) if any(s)),
    key=lambda s: -(far(s[0], NC) + far(s[1], NZ)),
)
CHIP_STEPS = (2, 1, 3, 0)
ROW_STEPS = ((2, 1), (2, 0), (1, 1), (3, 1), (1, 0), (3, 0), (0, 1))


def lanes(shape):
    return lax.broadcasted_iota(jnp.int32, shape, len(shape) - 1)


def rows(shape):
    return lax.broadcasted_iota(jnp.int32, shape, len(shape) - 2)


def roll(x, shift):
    shift %= x.shape[-1]
    return x if shift == 0 else pltpu.roll(x, shift, x.ndim - 1)


def kernel(
    pairs_hbm,
    slot_hbm,
    tag_hbm,
    levels_hbm,
    cen_hbm,
    exp_hbm,
    block_hbm,
    refs_hbm,
    cell_hbm,
    out_ref,
    pairs_ref,
    slot_ref,
    tag_ref,
    levels_ref,
    cen_ref,
    exp_ref,
    block_ref,
    refs_ref,
    cell_ref,
    colx_ref,
    colyz_ref,
    rowx_ref,
    rowyz_ref,
    dens_ref,
    a_out,
    a_got,
    h_out,
    h_got,
    r_out,
    r_got,
    b_out,
    b_got,
    c_out,
    c_got,
    load_sem,
    a_send,
    a_recv,
    h_send,
    h_recv,
    r_send,
    r_recv,
    b_send,
    b_recv,
    c_send,
    c_recv,
):
    loads = [
        pltpu.make_async_copy(source, into, load_sem.at[n])
        for n, (source, into) in enumerate(
            (
                (pairs_hbm, pairs_ref),
                (slot_hbm, slot_ref),
                (tag_hbm, tag_ref),
                (levels_hbm, levels_ref),
                (cen_hbm, cen_ref),
                (exp_hbm, exp_ref),
                (block_hbm, block_ref),
                (refs_hbm, refs_ref),
                (cell_hbm, cell_ref),
            )
        )
    ]
    r, y, z = (lax.axis_index(a) for a in ("row", "col", "basis"))
    ys = [lax.rem(y + n, NC) for n in range(NC)]
    zs = [lax.rem(z + n, NZ) for n in range(NZ)]
    x, core = r // 2, lax.rem(r, 2)
    xs = [lax.rem(x + n, NX) * 2 for n in range(NX)]
    cores = [core, 1 - core]
    row_of = [xs[dx] + cores[dc] for dx, dc in ROW_STEPS]
    me = y * NZ + z

    barrier = pltpu.get_barrier_semaphore()

    def entered(*device):
        pl.semaphore_signal(barrier, inc=1, device_id=device, device_id_type=MESH)

    for load in loads:
        load.start()
    for dy, dz in PLANE_STEPS:
        entered(r, ys[dy], zs[dz])
    for other in row_of:
        entered(other, y, z)

    step16 = rows((EDGE, BS)).astype(F32) - HALF
    lane256 = lanes((1, EDGE * EDGE))
    step_y = (lane256 // EDGE).astype(F32) - HALF
    step_z = (lane256 % EDGE).astype(F32) - HALF
    lane = lanes((ITEMS, 128))
    for load in loads:
        load.wait()

    numbers = jnp.zeros((ITEMS, 128), F32)
    spacings, params, row_xs = [], [], []
    for k in range(ITEMS):
        first, second = pairs_ref[0, k], pairs_ref[1, k]
        group, tag = slot_ref[k], tag_ref[k]
        spacing = jnp.where(levels_ref[group * GROUP + tag] == 0, 0.2, 0.1).astype(F32)
        spacings.append(spacing)
        place = (group & 7) * GROUP + tag
        number = (group >> 3) * OWN + (place & 1) * PLANE + (place >> 1)
        numbers = jnp.where(rows((ITEMS, 128)) == k, number.astype(F32), numbers)

        points = step16 * spacing
        rate = exp_ref[pl.ds(second, 1), :]
        middle = [cen_ref[d, pl.ds(second, 1), :] for d in range(3)]
        col_x, col_y, col_z = [jnp.exp(-rate * (points - m) ** 2) for m in middle]
        colx_ref[k] = col_x
        for n in range(EDGE):
            colyz_ref[k, n * EDGE : n * EDGE + EDGE, :] = col_y[n : n + 1] * col_z

        rate = exp_ref[pl.ds(first, 1), :]
        middle = [cen_ref[d, pl.ds(first, 1), :] for d in range(3)]
        row_xs.append(jnp.exp(-rate * (points - middle[0]) ** 2))
        params += [-rate, middle[1], middle[2]]
    columns = jnp.transpose(
        jnp.concatenate(params + [jnp.zeros((32 - 3 * ITEMS, BS), F32)], axis=0)
    )
    row_x = jnp.transpose(jnp.concatenate(row_xs, axis=0))
    for k in range(ITEMS):
        rowx_ref[k] = roll(row_x, -EDGE * k)
        decay, middle_y, middle_z = (columns[:, 3 * k + n : 3 * k + n + 1] for n in range(3))
        rowyz_ref[k] = jnp.exp(
            decay
            * (
                (step_y * spacings[k] - middle_y) ** 2
                + (step_z * spacings[k] - middle_z) ** 2
            )
        )

    def item(k, carry):
        block = block_ref[k]
        col_x = colx_ref[k]
        row_x = rowx_ref[k]
        for n in range(EDGE):
            col_values = (col_x[n : n + 1] * colyz_ref[k]).astype(BF16)
            product = lax.dot_general(block, col_values, NT, preferred_element_type=F32)
            weighted = product * rowyz_ref[k] * row_x[:, n : n + 1]
            dens_ref[pl.ds(k, 1), n * 256 : n * 256 + 256] = jnp.sum(
                weighted, axis=0, keepdims=True
            )
        return carry

    lax.fori_loop(0, ITEMS // 2, item, 0, unroll=True)
    lax.fori_loop(ITEMS // 2, ITEMS, item, 0, unroll=True)

    extra = jnp.where(lane == TARGET, numbers, 0.0)
    for c, q in enumerate(CORNERS):
        tile = dens_ref[:, q // 128 * 128 : q // 128 * 128 + 128]
        extra = jnp.where(lane == CORNER + c, roll(tile, CORNER + c - q), extra)
    lower = lane < 64

    def beside(x):
        return pltpu.roll(roll(x, 64), 4, 0)

    extra = jnp.where(lower, extra, beside(extra))
    point = (lane & 63) < SUB
    for t in range(PTS // 128):
        tile = dens_ref[:, t * 128 : t * 128 + 128]
        other = beside(tile)
        for m in range(3):
            value = jnp.where(lower, roll(tile, -SUB * m), roll(other, -SUB * m))
            a_out[3 * t + m] = jnp.where(point, value, extra)[:4]
    pl.semaphore_wait(barrier, PLANE + NR - 2)

    def plane_copies(out, got, send, recv):
        for dy, dz in PLANE_STEPS:
            pltpu.make_async_remote_copy(
                src_ref=out.at[ys[dy] * NZ + zs[dz]],
                dst_ref=got.at[me],
                send_sem=send,
                recv_sem=recv,
                device_id=(r, ys[dy], zs[dz]),
                device_id_type=MESH,
            ).start()
        got[me] = out[me]

    def arrived(ref, count, sem):
        whole = ref.at[pl.ds(0, count)]
        pltpu.make_async_copy(whole, whole, sem).wait()

    plane_copies(a_out, a_got, a_send, a_recv)
    arrived(a_got, PLANE - 1, a_recv)

    turned = jnp.transpose(
        jnp.concatenate([a_got[a] for a in range(PLANE)], axis=0)
    )
    values = jnp.concatenate([turned[:ROWS], turned[64 : 64 + ROWS]], axis=1)
    high = values.astype(BF16)
    low = (values - high.astype(F32)).astype(BF16)
    left = jnp.concatenate([high, low], axis=0)
    wanted = values[TARGET : TARGET + 1, :]
    count = rows((128, PLANE * ITEMS)).astype(F32)
    count2 = jnp.where(count < 64.0, count + 128.0, count + 64.0)
    half = lanes((32, 128)) < 64

    def table(row):
        here = wanted - (row * OWN).astype(F32)
        parts = []
        for at in (count, count2):
            right = jnp.where(at == here, 1.0, 0.0).astype(BF16)
            both = lax.dot_general(left, right, NT, preferred_element_type=F32)
            parts.append(both[:ROWS] + both[ROWS:])
        whole, mixed = parts
        mixed = jnp.concatenate([mixed, jnp.zeros((64 - ROWS, 128), F32)], axis=0)
        return jnp.concatenate([whole, jnp.where(half, mixed[:32], mixed[32:])], axis=0)

    halves = []
    for n, dx in enumerate(CHIP_STEPS):
        h_out[n] = table(xs[dx] + cores[1])
        half_copy = pltpu.make_async_remote_copy(
            src_ref=h_out.at[n],
            dst_ref=h_got.at[n],
            send_sem=h_send,
            recv_sem=h_recv.at[n],
            device_id=(xs[0] + cores[1], y, z),
            device_id_type=MESH,
        )
        half_copy.start()
        halves.append(half_copy)
    for n, dx in enumerate(CHIP_STEPS):
        r_out[n] = table(xs[dx] + core)
    for n, dx in enumerate(CHIP_STEPS[:-1]):
        halves[n].wait_recv()
        r_out[n] = r_out[n] + h_got[n]
        pltpu.make_async_remote_copy(
            src_ref=r_out.at[n],
            dst_ref=r_got.at[n],
            send_sem=r_send,
            recv_sem=r_recv,
            device_id=(xs[dx] + core, y, z),
            device_id_type=MESH,
        ).start()
    halves[-1].wait_recv()
    total = r_out[NX - 1] + h_got[NX - 1]
    arrived(r_got, NX - 1, r_recv)
    for n in range(NX - 1):
        total = total + r_got[n]
    whole, mixed = total[:ROWS], total[ROWS:]
    mixed = jnp.concatenate([mixed, roll(mixed, 64)], axis=0)

    c_out[:, :128] = whole[CORNER : CORNER + 8]
    c_out[:, 128:] = mixed[CORNER : CORNER + 8]
    for other in row_of:
        pltpu.make_async_remote_copy(
            src_ref=c_out,
            dst_ref=c_got.at[r],
            send_sem=c_send,
            recv_sem=c_recv,
            device_id=(other, y, z),
            device_id_type=MESH,
        ).start()
    c_got[r] = c_out[...]

    whole = jnp.concatenate([whole, jnp.zeros((64 - ROWS, 128), F32)], axis=0)
    second = jnp.where(lanes((64, 128)) < 32, roll(whole, 32), roll(mixed, 32))
    bricks = jnp.transpose(jnp.concatenate([whole, second], axis=0))
    for a in range(PLANE):
        b_out[a] = bricks[a : a + 1]
    plane_copies(b_out, b_got, b_send, b_recv)

    arrived(c_got, NR - 1, c_recv)
    kept, added = [], []
    for b in range(2):
        means = []
        for h in range(2):
            ref = refs_ref[b, :, h * 128 : h * 128 + 128]
            corner, brick = ref & 7, ref >> 3
            source = ((brick >> 6) * 11) >> 5
            place = brick - source * OWN
            place = (place >> 1) + (place & 1) * PLANE
            at = place & 127
            which = (source * 2 + (place >> 7)) * 8 + corner
            found = jnp.zeros((8, 128), F32)
            for n in range(NR):
                for part in range(2):
                    for c in range(8):
                        line = jnp.broadcast_to(
                            c_got[n, c : c + 1, part * 128 : part * 128 + 128], (8, 128)
                        )
                        here = jnp.take_along_axis(line, at, axis=1)
                        found = jnp.where(which == (n * 2 + part) * 8 + c, here, found)
            means.append(jnp.sum(found, axis=0, keepdims=True) * 0.0625)
        mean = jnp.concatenate(means, axis=1)
        cell = cell_ref[b : b + 1, :]
        upper = rows((32, 256)) == (cell >> 7)
        coarse = mean.astype(BF16).astype(F32)
        weights = jnp.concatenate(
            [
                jnp.where(upper, coarse, 0.0),
                jnp.where(upper, mean - coarse, 0.0),
                jnp.where(upper, 0.5, 0.0),
            ],
            axis=0,
        ).astype(BF16)
        spots = jnp.where(rows((128, 256)) == (cell & 127), 1.0, 0.0).astype(BF16)
        spread = lax.dot_general(weights, spots, NT, preferred_element_type=F32)
        added.append(spread[:32] + spread[32:64])
        kept.append(1.0 - spread[64:])

    arrived(b_got, PLANE - 1, b_recv)
    lane = lanes((1, 128))
    for b in range(2):
        for t in range(PTS // 128):
            thirds = [roll(b_got[3 * t + m], SUB * m - 64 * b) for m in range(3)]
            value = jnp.where(
                lane < SUB, thirds[0], jnp.where(lane < 2 * SUB, thirds[1], thirds[2])
            )
            out_ref[b : b + 1, t * 128 : t * 128 + 128] = (
                value * kept[b][t : t + 1] + added[b][t : t + 1]
            )
    arrived(a_out, PLANE - 1, a_send)
    arrived(h_out, NX, h_send)
    arrived(r_out, NX - 1, r_send)
    arrived(b_out, PLANE - 1, b_send)
    arrived(c_got, NR - 1, c_send)


def body(
    block_data, item_pairs, dest_slot, brick_tag, centres, exponents, levels, cell_pos, corner_refs
):
    arguments = (
        item_pairs.T,
        dest_slot,
        brick_tag,
        levels,
        centres.transpose(1, 0, 2),
        exponents,
        block_data,
        corner_refs.transpose(0, 2, 1),
        cell_pos,
    )
    places = [pltpu.SMEM] * 4 + [pltpu.VMEM] * 5
    dma = pltpu.SemaphoreType.DMA
    return pl.pallas_call(
        kernel,
        out_shape=pltpu.VMEM((2, PTS), F32),
        in_specs=[pl.BlockSpec(memory_space=pltpu.HBM)] * len(arguments),
        out_specs=pl.BlockSpec(memory_space=pltpu.VMEM),
        scratch_shapes=[place(a.shape, a.dtype) for place, a in zip(places, arguments)]
        + [
            pltpu.VMEM((ITEMS, EDGE, BS), F32),
            pltpu.VMEM((ITEMS, EDGE * EDGE, BS), F32),
            pltpu.VMEM((ITEMS, BS, 128), F32),
            pltpu.VMEM((ITEMS, BS, EDGE * EDGE), F32),
            pltpu.VMEM((ITEMS, PTS), F32),
            pltpu.VMEM((PLANE, 4, 128), F32),
            pltpu.VMEM((PLANE, 4, 128), F32),
            pltpu.VMEM((NX, ROWS + 32, 128), F32),
            pltpu.VMEM((NX, ROWS + 32, 128), F32),
            pltpu.VMEM((NX, ROWS + 32, 128), F32),
            pltpu.VMEM((NX - 1, ROWS + 32, 128), F32),
            pltpu.VMEM((PLANE, 1, 128), F32),
            pltpu.VMEM((PLANE, 1, 128), F32),
            pltpu.VMEM((8, 256), F32),
            pltpu.VMEM((NR, 8, 256), F32),
            dma((len(arguments),)),
        ]
        + [dma, dma, dma, dma((NX,))]
        + [dma] * 6,
        compiler_params=pltpu.CompilerParams(
            collective_id=0, has_side_effects=True, vmem_limit_bytes=60 * 2**20
        ),
        name="collocate",
    )(*arguments)


def solution(mesh):
    spread = ("row", "col", "basis")
    return jax.shard_map(
        body,
        mesh=mesh,
        in_specs=(
            P(spread, None, None),
            P(spread, None),
            P(spread),
            P(spread),
            P(),
            P(),
            P(),
            P(spread, None),
            P(spread, None, None),
        ),
        out_specs=P(spread, None),
        check_vma=False,
    )
```

```python
import itertools

import jax
import jax.numpy as jnp
from jax import lax
from jax.experimental import pallas as pl
from jax.experimental.pallas import tpu as pltpu
from jax.sharding import PartitionSpec as P

MESH = pl.DeviceIdType.MESH
F32 = jnp.float32
BF16 = jnp.bfloat16

EDGE = 16
HALF = (EDGE - 1) / 2.0
PTS = EDGE**3
BS = 128
ITEMS = 8
NR, NC, NZ = 8, 8, 12
NX = NR // 2
PLANE = NC * NZ
BATCH = 24
GROUP = 24
OWN = NC * GROUP
SUB = 43
TARGET = SUB
CORNER = 48
ROWS = 56
NT = (((1,), (1,)), ((), ()))
CORNERS = tuple(
    ((c // 4) * 15 * EDGE + (c // 2 % 2) * 15) * EDGE + (c % 2) * 15 for c in range(8)
)


def far(step, size):
    return min(step, size - step)


PLANE_STEPS = sorted(
    (s for s in itertools.product(range(NC), range(NZ)) if any(s)),
    key=lambda s: -(far(s[0], NC) + far(s[1], NZ)),
)
CHIP_STEPS = (2, 1, 3, 0)
ROW_STEPS = ((2, 1), (2, 0), (1, 1), (3, 1), (1, 0), (3, 0), (0, 1))


def lanes(shape):
    return lax.broadcasted_iota(jnp.int32, shape, len(shape) - 1)


def rows(shape):
    return lax.broadcasted_iota(jnp.int32, shape, len(shape) - 2)


def roll(x, shift):
    shift %= x.shape[-1]
    return x if shift == 0 else pltpu.roll(x, shift, x.ndim - 1)


def kernel(
    pairs_hbm,
    slot_hbm,
    tag_hbm,
    levels_hbm,
    cen_hbm,
    exp_hbm,
    block_hbm,
    refs_hbm,
    cell_hbm,
    out_ref,
    pairs_ref,
    slot_ref,
    tag_ref,
    levels_ref,
    cen_ref,
    exp_ref,
    block_ref,
    refs_ref,
    cell_ref,
    colx_ref,
    colyz_ref,
    rowx_ref,
    rowyz_ref,
    dens_ref,
    side_ref,
    bricks_ref,
    a_out,
    a_got,
    h_out,
    h_got,
    r_out,
    r_got,
    b_out,
    b_got,
    c_out,
    c_got,
    load_sem,
    a_send,
    a_recv,
    h_send,
    h_recv,
    r_send,
    r_recv,
    b_send,
    b_recv,
    c_send,
    c_recv,
):
    loads = [
        pltpu.make_async_copy(source, into, load_sem.at[n])
        for n, (source, into) in enumerate(
            (
                (pairs_hbm, pairs_ref),
                (slot_hbm, slot_ref),
                (tag_hbm, tag_ref),
                (levels_hbm, levels_ref),
                (cen_hbm, cen_ref),
                (exp_hbm, exp_ref),
                (block_hbm, block_ref),
                (refs_hbm, refs_ref),
                (cell_hbm, cell_ref),
            )
        )
    ]
    r, y, z = (lax.axis_index(a) for a in ("row", "col", "basis"))
    ys = [lax.rem(y + n, NC) for n in range(NC)]
    zs = [lax.rem(z + n, NZ) for n in range(NZ)]
    x, core = r // 2, lax.rem(r, 2)
    xs = [lax.rem(x + n, NX) * 2 for n in range(NX)]
    cores = [core, 1 - core]
    row_of = [xs[dx] + cores[dc] for dx, dc in ROW_STEPS]
    me = y * NZ + z

    barrier = pltpu.get_barrier_semaphore()

    def entered(*device):
        pl.semaphore_signal(barrier, inc=1, device_id=device, device_id_type=MESH)

    for load in loads:
        load.start()
    for dy, dz in PLANE_STEPS:
        entered(r, ys[dy], zs[dz])
    for other in row_of:
        entered(other, y, z)

    step16 = rows((EDGE, BS)).astype(F32) - HALF
    lane256 = lanes((1, EDGE * EDGE))
    step_y = (lane256 // EDGE).astype(F32) - HALF
    step_z = (lane256 % EDGE).astype(F32) - HALF
    lane = lanes((ITEMS, 128))
    for load in loads:
        load.wait()

    numbers = jnp.zeros((ITEMS, 128), F32)
    spacings, params, row_xs = [], [], []
    for k in range(ITEMS):
        first, second = pairs_ref[0, k], pairs_ref[1, k]
        group, tag = slot_ref[k], tag_ref[k]
        spacing = jnp.where(levels_ref[group * GROUP + tag] == 0, 0.2, 0.1).astype(F32)
        spacings.append(spacing)
        place = (group & 7) * GROUP + tag
        number = (group >> 3) * OWN + (place & 1) * PLANE + (place >> 1)
        numbers = jnp.where(rows((ITEMS, 128)) == k, number.astype(F32), numbers)

        points = step16 * spacing
        rate = exp_ref[pl.ds(second, 1), :]
        middle = [cen_ref[d, pl.ds(second, 1), :] for d in range(3)]
        col_x, col_y, col_z = [jnp.exp(-rate * (points - m) ** 2) for m in middle]
        colx_ref[k] = col_x
        for n in range(EDGE):
            colyz_ref[k, n * EDGE : n * EDGE + EDGE, :] = col_y[n : n + 1] * col_z

        rate = exp_ref[pl.ds(first, 1), :]
        middle = [cen_ref[d, pl.ds(first, 1), :] for d in range(3)]
        row_xs.append(jnp.exp(-rate * (points - middle[0]) ** 2))
        params += [-rate, middle[1], middle[2]]
    columns = jnp.transpose(
        jnp.concatenate(params + [jnp.zeros((32 - 3 * ITEMS, BS), F32)], axis=0)
    )
    row_x = jnp.transpose(jnp.concatenate(row_xs, axis=0))
    for k in range(ITEMS):
        rowx_ref[k] = roll(row_x, -EDGE * k)
        decay, middle_y, middle_z = (columns[:, 3 * k + n : 3 * k + n + 1] for n in range(3))
        rowyz_ref[k] = jnp.exp(
            decay
            * (
                (step_y * spacings[k] - middle_y) ** 2
                + (step_z * spacings[k] - middle_z) ** 2
            )
        )

    def item(k, carry):
        block = block_ref[k]
        col_x = colx_ref[k]
        row_x = rowx_ref[k]
        for n in range(EDGE):
            col_values = (col_x[n : n + 1] * colyz_ref[k]).astype(BF16)
            product = lax.dot_general(block, col_values, NT, preferred_element_type=F32)
            weighted = product * rowyz_ref[k] * row_x[:, n : n + 1]
            dens_ref[pl.ds(k, 1), n * 256 : n * 256 + 256] = jnp.sum(
                weighted, axis=0, keepdims=True
            )
        return carry

    lax.fori_loop(0, ITEMS // 2, item, 0, unroll=True)
    lax.fori_loop(ITEMS // 2, ITEMS, item, 0, unroll=True)

    extra = jnp.where(lane == TARGET, numbers, 0.0)
    for c, q in enumerate(CORNERS):
        tile = dens_ref[:, q // 128 * 128 : q // 128 * 128 + 128]
        extra = jnp.where(lane == CORNER + c, roll(tile, CORNER + c - q), extra)
    lower = lane < 64

    def beside(x):
        return pltpu.roll(roll(x, 64), 4, 0)

    extra = jnp.where(lower, extra, beside(extra))
    point = (lane & 63) < SUB
    for t in range(PTS // 128):
        side_ref[:, t * 128 : t * 128 + 128] = beside(dens_ref[:, t * 128 : t * 128 + 128])
    tiles_y = [n * (NZ // 3) for n in ys]
    tiles_z = [n // 3 for n in zs]
    turns = [lax.rem(128 - SUB * lax.rem(n, 3), 128) for n in zs]

    def chunk(dy, dz):
        at = pl.ds(pl.multiple_of((tiles_y[dy] + tiles_z[dz]) * 128, 128), 128)
        value = jnp.where(
            lower,
            pltpu.roll(dens_ref[:, at], turns[dz], 1),
            pltpu.roll(side_ref[:, at], turns[dz], 1),
        )
        return jnp.where(point, value, extra)[:4]

    def plane_copies(made, out, got, send, recv):
        for begin in range(0, PLANE - 1, BATCH):
            batch = list(enumerate(PLANE_STEPS))[begin : begin + BATCH]
            for n, (dy, dz) in batch:
                out[n] = made(dy, dz)
            for n, (dy, dz) in batch:
                pltpu.make_async_remote_copy(
                    src_ref=out.at[n],
                    dst_ref=got.at[me],
                    send_sem=send,
                    recv_sem=recv,
                    device_id=(r, ys[dy], zs[dz]),
                    device_id_type=MESH,
                ).start()
        got[me] = made(0, 0)

    def arrived(ref, count, sem):
        whole = ref.at[pl.ds(0, count)]
        pltpu.make_async_copy(whole, whole, sem).wait()

    pl.semaphore_wait(barrier, PLANE + NR - 2)
    plane_copies(chunk, a_out, a_got, a_send, a_recv)
    arrived(a_got, PLANE - 1, a_recv)

    turned = jnp.transpose(
        jnp.concatenate([a_got[a] for a in range(PLANE)], axis=0)
    )
    values = jnp.concatenate([turned[:ROWS], turned[64 : 64 + ROWS]], axis=1)
    high = values.astype(BF16)
    low = (values - high.astype(F32)).astype(BF16)
    left = jnp.concatenate([high, low], axis=0)
    wanted = values[TARGET : TARGET + 1, :]
    count = rows((128, PLANE * ITEMS)).astype(F32)
    count2 = jnp.where(count < 64.0, count + 128.0, count + 64.0)
    half = lanes((32, 128)) < 64

    def table(row):
        here = wanted - (row * OWN).astype(F32)
        parts = []
        for at in (count, count2):
            right = jnp.where(at == here, 1.0, 0.0).astype(BF16)
            both = lax.dot_general(left, right, NT, preferred_element_type=F32)
            parts.append(both[:ROWS] + both[ROWS:])
        whole, mixed = parts
        mixed = jnp.concatenate([mixed, jnp.zeros((64 - ROWS, 128), F32)], axis=0)
        return jnp.concatenate([whole, jnp.where(half, mixed[:32], mixed[32:])], axis=0)

    halves = []
    for n, dx in enumerate(CHIP_STEPS):
        h_out[n] = table(xs[dx] + cores[1])
        half_copy = pltpu.make_async_remote_copy(
            src_ref=h_out.at[n],
            dst_ref=h_got.at[n],
            send_sem=h_send,
            recv_sem=h_recv.at[n],
            device_id=(xs[0] + cores[1], y, z),
            device_id_type=MESH,
        )
        half_copy.start()
        halves.append(half_copy)
    for n, dx in enumerate(CHIP_STEPS):
        r_out[n] = table(xs[dx] + core)
    for n, dx in enumerate(CHIP_STEPS[:-1]):
        halves[n].wait_recv()
        r_out[n] = r_out[n] + h_got[n]
        pltpu.make_async_remote_copy(
            src_ref=r_out.at[n],
            dst_ref=r_got.at[n],
            send_sem=r_send,
            recv_sem=r_recv,
            device_id=(xs[dx] + core, y, z),
            device_id_type=MESH,
        ).start()
    halves[-1].wait_recv()
    total = r_out[NX - 1] + h_got[NX - 1]
    arrived(r_got, NX - 1, r_recv)
    for n in range(NX - 1):
        total = total + r_got[n]
    whole, mixed = total[:ROWS], total[ROWS:]
    mixed = jnp.concatenate([mixed, roll(mixed, 64)], axis=0)

    c_out[:, :128] = whole[CORNER : CORNER + 8]
    c_out[:, 128:] = mixed[CORNER : CORNER + 8]
    for other in row_of:
        pltpu.make_async_remote_copy(
            src_ref=c_out,
            dst_ref=c_got.at[r],
            send_sem=c_send,
            recv_sem=c_recv,
            device_id=(other, y, z),
            device_id_type=MESH,
        ).start()
    c_got[r] = c_out[...]

    whole = jnp.concatenate([whole, jnp.zeros((64 - ROWS, 128), F32)], axis=0)
    second = jnp.where(lanes((64, 128)) < 32, roll(whole, 32), roll(mixed, 32))
    bricks_ref[...] = jnp.transpose(jnp.concatenate([whole, second], axis=0))

    def own_points(dy, dz):
        return bricks_ref[pl.ds(ys[dy] * NZ + zs[dz], 1), :]

    plane_copies(own_points, b_out, b_got, b_send, b_recv)

    arrived(c_got, NR - 1, c_recv)
    kept, added = [], []
    for b in range(2):
        means = []
        for h in range(2):
            ref = refs_ref[b, :, h * 128 : h * 128 + 128]
            corner, brick = ref & 7, ref >> 3
            source = ((brick >> 6) * 11) >> 5
            place = brick - source * OWN
            place = (place >> 1) + (place & 1) * PLANE
            at = place & 127
            which = (source * 2 + (place >> 7)) * 8 + corner
            found = jnp.zeros((8, 128), F32)
            for n in range(NR):
                for part in range(2):
                    for c in range(8):
                        line = jnp.broadcast_to(
                            c_got[n, c : c + 1, part * 128 : part * 128 + 128], (8, 128)
                        )
                        here = jnp.take_along_axis(line, at, axis=1)
                        found = jnp.where(which == (n * 2 + part) * 8 + c, here, found)
            means.append(jnp.sum(found, axis=0, keepdims=True) * 0.0625)
        mean = jnp.concatenate(means, axis=1)
        cell = cell_ref[b : b + 1, :]
        upper = rows((32, 256)) == (cell >> 7)
        coarse = mean.astype(BF16).astype(F32)
        weights = jnp.concatenate(
            [
                jnp.where(upper, coarse, 0.0),
                jnp.where(upper, mean - coarse, 0.0),
                jnp.where(upper, 0.5, 0.0),
            ],
            axis=0,
        ).astype(BF16)
        spots = jnp.where(rows((128, 256)) == (cell & 127), 1.0, 0.0).astype(BF16)
        spread = lax.dot_general(weights, spots, NT, preferred_element_type=F32)
        added.append(spread[:32] + spread[32:64])
        kept.append(1.0 - spread[64:])

    arrived(b_got, PLANE - 1, b_recv)
    lane = lanes((1, 128))
    for b in range(2):
        for t in range(PTS // 128):
            thirds = [roll(b_got[3 * t + m], SUB * m - 64 * b) for m in range(3)]
            value = jnp.where(
                lane < SUB, thirds[0], jnp.where(lane < 2 * SUB, thirds[1], thirds[2])
            )
            out_ref[b : b + 1, t * 128 : t * 128 + 128] = (
                value * kept[b][t : t + 1] + added[b][t : t + 1]
            )
    arrived(a_out, PLANE - 1, a_send)
    arrived(h_out, NX, h_send)
    arrived(r_out, NX - 1, r_send)
    arrived(b_out, PLANE - 1, b_send)
    arrived(c_got, NR - 1, c_send)


def body(
    block_data, item_pairs, dest_slot, brick_tag, centres, exponents, levels, cell_pos, corner_refs
):
    arguments = (
        item_pairs.T,
        dest_slot,
        brick_tag,
        levels,
        centres.transpose(1, 0, 2),
        exponents,
        block_data,
        corner_refs.transpose(0, 2, 1),
        cell_pos,
    )
    places = [pltpu.SMEM] * 4 + [pltpu.VMEM] * 5
    dma = pltpu.SemaphoreType.DMA
    return pl.pallas_call(
        kernel,
        out_shape=pltpu.VMEM((2, PTS), F32),
        in_specs=[pl.BlockSpec(memory_space=pltpu.HBM)] * len(arguments),
        out_specs=pl.BlockSpec(memory_space=pltpu.VMEM),
        scratch_shapes=[place(a.shape, a.dtype) for place, a in zip(places, arguments)]
        + [
            pltpu.VMEM((ITEMS, EDGE, BS), F32),
            pltpu.VMEM((ITEMS, EDGE * EDGE, BS), F32),
            pltpu.VMEM((ITEMS, BS, 128), F32),
            pltpu.VMEM((ITEMS, BS, EDGE * EDGE), F32),
            pltpu.VMEM((ITEMS, PTS), F32),
            pltpu.VMEM((ITEMS, PTS), F32),
            pltpu.VMEM((128, 128), F32),
            pltpu.VMEM((PLANE - 1, 4, 128), F32),
            pltpu.VMEM((PLANE, 4, 128), F32),
            pltpu.VMEM((NX, ROWS + 32, 128), F32),
            pltpu.VMEM((NX, ROWS + 32, 128), F32),
            pltpu.VMEM((NX, ROWS + 32, 128), F32),
            pltpu.VMEM((NX - 1, ROWS + 32, 128), F32),
            pltpu.VMEM((PLANE - 1, 1, 128), F32),
            pltpu.VMEM((PLANE, 1, 128), F32),
            pltpu.VMEM((8, 256), F32),
            pltpu.VMEM((NR, 8, 256), F32),
            dma((len(arguments),)),
        ]
        + [dma, dma, dma, dma((NX,))]
        + [dma] * 6,
        compiler_params=pltpu.CompilerParams(
            collective_id=0, has_side_effects=True, vmem_limit_bytes=60 * 2**20
        ),
        name="collocate",
    )(*arguments)


def solution(mesh):
    spread = ("row", "col", "basis")
    return jax.shard_map(
        body,
        mesh=mesh,
        in_specs=(
            P(spread, None, None),
            P(spread, None),
            P(spread),
            P(spread),
            P(),
            P(),
            P(),
            P(spread, None),
            P(spread, None, None),
        ),
        out_specs=P(spread, None),
        check_vma=False,
    )
```

```python
import itertools

import jax
import jax.numpy as jnp
from jax import lax
from jax.experimental import pallas as pl
from jax.experimental.pallas import tpu as pltpu
from jax.sharding import PartitionSpec as P

MESH = pl.DeviceIdType.MESH
F32 = jnp.float32
BF16 = jnp.bfloat16

EDGE = 16
HALF = (EDGE - 1) / 2.0
PTS = EDGE**3
BS = 128
ITEMS = 8
NR, NC, NZ = 8, 8, 12
NX = NR // 2
PLANE = NC * NZ
BATCH = 24
GROUP = 24
OWN = NC * GROUP
SUB = 43
TARGET = SUB
CORNER = 48
ROWS = 56
NT = (((1,), (1,)), ((), ()))
CORNERS = tuple(
    ((c // 4) * 15 * EDGE + (c // 2 % 2) * 15) * EDGE + (c % 2) * 15 for c in range(8)
)


def far(step, size):
    return min(step, size - step)


PLANE_STEPS = sorted(
    (s for s in itertools.product(range(NC), range(NZ)) if any(s)),
    key=lambda s: -(far(s[0], NC) + far(s[1], NZ)),
)
CHIP_STEPS = (2, 1, 3, 0)
ROW_STEPS = ((2, 1), (2, 0), (1, 1), (3, 1), (1, 0), (3, 0), (0, 1))


def lanes(shape):
    return lax.broadcasted_iota(jnp.int32, shape, len(shape) - 1)


def rows(shape):
    return lax.broadcasted_iota(jnp.int32, shape, len(shape) - 2)


def roll(x, shift):
    shift %= x.shape[-1]
    return x if shift == 0 else pltpu.roll(x, shift, x.ndim - 1)


def kernel(
    pairs_hbm,
    slot_hbm,
    tag_hbm,
    levels_hbm,
    cen_hbm,
    exp_hbm,
    block_hbm,
    refs_hbm,
    cell_hbm,
    out_ref,
    pairs_ref,
    slot_ref,
    tag_ref,
    levels_ref,
    cen_ref,
    exp_ref,
    block_ref,
    refs_ref,
    cell_ref,
    colx_ref,
    colyz_ref,
    rowx_ref,
    rowyz_ref,
    dens_ref,
    side_ref,
    bricks_ref,
    a_out,
    a_got,
    h_out,
    h_got,
    r_out,
    r_got,
    b_out,
    b_got,
    c_out,
    c_got,
    load_sem,
    a_send,
    a_recv,
    h_send,
    h_recv,
    r_send,
    r_recv,
    b_send,
    b_recv,
    c_send,
    c_recv,
):
    loads = [
        pltpu.make_async_copy(source, into, load_sem.at[n])
        for n, (source, into) in enumerate(
            (
                (pairs_hbm, pairs_ref),
                (slot_hbm, slot_ref),
                (tag_hbm, tag_ref),
                (levels_hbm, levels_ref),
                (cen_hbm, cen_ref),
                (exp_hbm, exp_ref),
                (block_hbm, block_ref),
                (refs_hbm, refs_ref),
                (cell_hbm, cell_ref),
            )
        )
    ]
    r, y, z = (lax.axis_index(a) for a in ("row", "col", "basis"))
    ys = [lax.rem(y + n, NC) for n in range(NC)]
    zs = [lax.rem(z + n, NZ) for n in range(NZ)]
    x, core = r // 2, lax.rem(r, 2)
    xs = [lax.rem(x + n, NX) * 2 for n in range(NX)]
    cores = [core, 1 - core]
    row_of = [xs[dx] + cores[dc] for dx, dc in ROW_STEPS]
    me = y * NZ + z

    barrier = pltpu.get_barrier_semaphore()

    def entered(*device):
        pl.semaphore_signal(barrier, inc=1, device_id=device, device_id_type=MESH)

    for dy, dz in PLANE_STEPS[:BATCH]:
        entered(r, ys[dy], zs[dz])
    for load in loads:
        load.start()
    for dy, dz in PLANE_STEPS[BATCH:]:
        entered(r, ys[dy], zs[dz])
    for other in row_of:
        entered(other, y, z)

    step16 = rows((EDGE, BS)).astype(F32) - HALF
    lane256 = lanes((1, EDGE * EDGE))
    step_y = (lane256 // EDGE).astype(F32) - HALF
    step_z = (lane256 % EDGE).astype(F32) - HALF
    lane = lanes((ITEMS, 128))
    for load in loads:
        load.wait()

    numbers = jnp.zeros((ITEMS, 128), F32)
    spacings, params, row_xs = [], [], []
    for k in range(ITEMS):
        first, second = pairs_ref[0, k], pairs_ref[1, k]
        group, tag = slot_ref[k], tag_ref[k]
        spacing = jnp.where(levels_ref[group * GROUP + tag] == 0, 0.2, 0.1).astype(F32)
        spacings.append(spacing)
        place = (group & 7) * GROUP + tag
        number = (group >> 3) * OWN + (place & 1) * PLANE + (place >> 1)
        numbers = jnp.where(rows((ITEMS, 128)) == k, number.astype(F32), numbers)

        points = step16 * spacing
        rate = exp_ref[pl.ds(second, 1), :]
        middle = [cen_ref[d, pl.ds(second, 1), :] for d in range(3)]
        col_x, col_y, col_z = [jnp.exp(-rate * (points - m) ** 2) for m in middle]
        colx_ref[k] = col_x
        for n in range(EDGE):
            colyz_ref[k, n * EDGE : n * EDGE + EDGE, :] = col_y[n : n + 1] * col_z

        rate = exp_ref[pl.ds(first, 1), :]
        middle = [cen_ref[d, pl.ds(first, 1), :] for d in range(3)]
        row_xs.append(jnp.exp(-rate * (points - middle[0]) ** 2))
        params += [-rate, middle[1], middle[2]]
    columns = jnp.transpose(
        jnp.concatenate(params + [jnp.zeros((32 - 3 * ITEMS, BS), F32)], axis=0)
    )
    row_x = jnp.transpose(jnp.concatenate(row_xs, axis=0))
    for k in range(ITEMS):
        rowx_ref[k] = roll(row_x, -EDGE * k)
        decay, middle_y, middle_z = (columns[:, 3 * k + n : 3 * k + n + 1] for n in range(3))
        rowyz_ref[k] = jnp.exp(
            decay
            * (
                (step_y * spacings[k] - middle_y) ** 2
                + (step_z * spacings[k] - middle_z) ** 2
            )
        )

    def item(k, carry):
        block = block_ref[k]
        col_x = colx_ref[k]
        row_x = rowx_ref[k]
        for n in range(EDGE):
            col_values = (col_x[n : n + 1] * colyz_ref[k]).astype(BF16)
            product = lax.dot_general(block, col_values, NT, preferred_element_type=F32)
            weighted = product * rowyz_ref[k] * row_x[:, n : n + 1]
            dens_ref[pl.ds(k, 1), n * 256 : n * 256 + 256] = jnp.sum(
                weighted, axis=0, keepdims=True
            )
        return carry

    lax.fori_loop(0, ITEMS // 2, item, 0, unroll=True)
    lax.fori_loop(ITEMS // 2, ITEMS, item, 0, unroll=True)

    extra = jnp.where(lane == TARGET, numbers, 0.0)
    for c, q in enumerate(CORNERS):
        tile = dens_ref[:, q // 128 * 128 : q // 128 * 128 + 128]
        extra = jnp.where(lane == CORNER + c, roll(tile, CORNER + c - q), extra)
    lower = lane < 64

    def beside(x):
        return pltpu.roll(roll(x, 64), 4, 0)

    extra = jnp.where(lower, extra, beside(extra))
    point = (lane & 63) < SUB
    for t in range(PTS // 128):
        side_ref[:, t * 128 : t * 128 + 128] = beside(dens_ref[:, t * 128 : t * 128 + 128])
    tiles_y = [n * (NZ // 3) for n in ys]
    tiles_z = [n // 3 for n in zs]
    turns = [lax.rem(128 - SUB * lax.rem(n, 3), 128) for n in zs]

    def chunk(dy, dz):
        at = pl.ds(pl.multiple_of((tiles_y[dy] + tiles_z[dz]) * 128, 128), 128)
        value = jnp.where(
            lower,
            pltpu.roll(dens_ref[:, at], turns[dz], 1),
            pltpu.roll(side_ref[:, at], turns[dz], 1),
        )
        return jnp.where(point, value, extra)[:4]

    def plane_copies(made, out, got, send, recv):
        for begin in range(0, PLANE - 1, BATCH):
            batch = list(enumerate(PLANE_STEPS))[begin : begin + BATCH]
            for n, (dy, dz) in batch:
                out[n] = made(dy, dz)
            for n, (dy, dz) in batch:
                pltpu.make_async_remote_copy(
                    src_ref=out.at[n],
                    dst_ref=got.at[me],
                    send_sem=send,
                    recv_sem=recv,
                    device_id=(r, ys[dy], zs[dz]),
                    device_id_type=MESH,
                ).start()
        got[me] = made(0, 0)

    def arrived(ref, count, sem):
        whole = ref.at[pl.ds(0, count)]
        pltpu.make_async_copy(whole, whole, sem).wait()

    pl.semaphore_wait(barrier, PLANE + NR - 2)
    plane_copies(chunk, a_out, a_got, a_send, a_recv)
    arrived(a_got, PLANE - 1, a_recv)

    turned = jnp.transpose(
        jnp.concatenate([a_got[a] for a in range(PLANE)], axis=0)
    )
    values = jnp.concatenate([turned[:ROWS], turned[64 : 64 + ROWS]], axis=1)
    high = values.astype(BF16)
    low = (values - high.astype(F32)).astype(BF16)
    left = jnp.concatenate([high, low], axis=0)
    wanted = values[TARGET : TARGET + 1, :]
    count = rows((128, PLANE * ITEMS)).astype(F32)
    count2 = jnp.where(count < 64.0, count + 128.0, count + 64.0)
    half = lanes((32, 128)) < 64

    def table(row):
        here = wanted - (row * OWN).astype(F32)
        parts = []
        for at in (count, count2):
            right = jnp.where(at == here, 1.0, 0.0).astype(BF16)
            both = lax.dot_general(left, right, NT, preferred_element_type=F32)
            parts.append(both[:ROWS] + both[ROWS:])
        whole, mixed = parts
        mixed = jnp.concatenate([mixed, jnp.zeros((64 - ROWS, 128), F32)], axis=0)
        return jnp.concatenate([whole, jnp.where(half, mixed[:32], mixed[32:])], axis=0)

    halves = []
    for n, dx in enumerate(CHIP_STEPS):
        h_out[n] = table(xs[dx] + cores[1])
        half_copy = pltpu.make_async_remote_copy(
            src_ref=h_out.at[n],
            dst_ref=h_got.at[n],
            send_sem=h_send,
            recv_sem=h_recv.at[n],
            device_id=(xs[0] + cores[1], y, z),
            device_id_type=MESH,
        )
        half_copy.start()
        halves.append(half_copy)
    for n, dx in enumerate(CHIP_STEPS):
        r_out[n] = table(xs[dx] + core)
    for n, dx in enumerate(CHIP_STEPS[:-1]):
        halves[n].wait_recv()
        r_out[n] = r_out[n] + h_got[n]
        pltpu.make_async_remote_copy(
            src_ref=r_out.at[n],
            dst_ref=r_got.at[n],
            send_sem=r_send,
            recv_sem=r_recv,
            device_id=(xs[dx] + core, y, z),
            device_id_type=MESH,
        ).start()
    halves[-1].wait_recv()
    total = r_out[NX - 1] + h_got[NX - 1]
    arrived(r_got, NX - 1, r_recv)
    for n in range(NX - 1):
        total = total + r_got[n]
    whole, mixed = total[:ROWS], total[ROWS:]
    mixed = jnp.concatenate([mixed, roll(mixed, 64)], axis=0)

    c_out[:, :128] = whole[CORNER : CORNER + 8]
    c_out[:, 128:] = mixed[CORNER : CORNER + 8]
    for other in row_of:
        pltpu.make_async_remote_copy(
            src_ref=c_out,
            dst_ref=c_got.at[r],
            send_sem=c_send,
            recv_sem=c_recv,
            device_id=(other, y, z),
            device_id_type=MESH,
        ).start()
    c_got[r] = c_out[...]

    whole = jnp.concatenate([whole, jnp.zeros((64 - ROWS, 128), F32)], axis=0)
    second = jnp.where(lanes((64, 128)) < 32, roll(whole, 32), roll(mixed, 32))
    bricks_ref[...] = jnp.transpose(jnp.concatenate([whole, second], axis=0))

    def own_points(dy, dz):
        return bricks_ref[pl.ds(ys[dy] * NZ + zs[dz], 1), :]

    plane_copies(own_points, b_out, b_got, b_send, b_recv)

    arrived(c_got, NR - 1, c_recv)
    kept, added = [], []
    for b in range(2):
        means = []
        for h in range(2):
            ref = refs_ref[b, :, h * 128 : h * 128 + 128]
            corner, brick = ref & 7, ref >> 3
            source = ((brick >> 6) * 11) >> 5
            place = brick - source * OWN
            place = (place >> 1) + (place & 1) * PLANE
            at = place & 127
            which = (source * 2 + (place >> 7)) * 8 + corner
            found = jnp.zeros((8, 128), F32)
            for n in range(NR):
                for part in range(2):
                    for c in range(8):
                        line = jnp.broadcast_to(
                            c_got[n, c : c + 1, part * 128 : part * 128 + 128], (8, 128)
                        )
                        here = jnp.take_along_axis(line, at, axis=1)
                        found = jnp.where(which == (n * 2 + part) * 8 + c, here, found)
            means.append(jnp.sum(found, axis=0, keepdims=True) * 0.0625)
        mean = jnp.concatenate(means, axis=1)
        cell = cell_ref[b : b + 1, :]
        upper = rows((32, 256)) == (cell >> 7)
        coarse = mean.astype(BF16).astype(F32)
        weights = jnp.concatenate(
            [
                jnp.where(upper, coarse, 0.0),
                jnp.where(upper, mean - coarse, 0.0),
                jnp.where(upper, 0.5, 0.0),
            ],
            axis=0,
        ).astype(BF16)
        spots = jnp.where(rows((128, 256)) == (cell & 127), 1.0, 0.0).astype(BF16)
        spread = lax.dot_general(weights, spots, NT, preferred_element_type=F32)
        added.append(spread[:32] + spread[32:64])
        kept.append(1.0 - spread[64:])

    arrived(b_got, PLANE - 1, b_recv)
    lane = lanes((1, 128))
    for b in range(2):
        for t in range(PTS // 128):
            thirds = [roll(b_got[3 * t + m], SUB * m - 64 * b) for m in range(3)]
            value = jnp.where(
                lane < SUB, thirds[0], jnp.where(lane < 2 * SUB, thirds[1], thirds[2])
            )
            out_ref[b : b + 1, t * 128 : t * 128 + 128] = (
                value * kept[b][t : t + 1] + added[b][t : t + 1]
            )
    arrived(a_out, PLANE - 1, a_send)
    arrived(h_out, NX, h_send)
    arrived(r_out, NX - 1, r_send)
    arrived(b_out, PLANE - 1, b_send)
    arrived(c_got, NR - 1, c_send)


def body(
    block_data, item_pairs, dest_slot, brick_tag, centres, exponents, levels, cell_pos, corner_refs
):
    arguments = (
        item_pairs.T,
        dest_slot,
        brick_tag,
        levels,
        centres.transpose(1, 0, 2),
        exponents,
        block_data,
        corner_refs.transpose(0, 2, 1),
        cell_pos,
    )
    places = [pltpu.SMEM] * 4 + [pltpu.VMEM] * 5
    dma = pltpu.SemaphoreType.DMA
    return pl.pallas_call(
        kernel,
        out_shape=pltpu.VMEM((2, PTS), F32),
        in_specs=[pl.BlockSpec(memory_space=pltpu.HBM)] * len(arguments),
        out_specs=pl.BlockSpec(memory_space=pltpu.VMEM),
        scratch_shapes=[place(a.shape, a.dtype) for place, a in zip(places, arguments)]
        + [
            pltpu.VMEM((ITEMS, EDGE, BS), F32),
            pltpu.VMEM((ITEMS, EDGE * EDGE, BS), F32),
            pltpu.VMEM((ITEMS, BS, 128), F32),
            pltpu.VMEM((ITEMS, BS, EDGE * EDGE), F32),
            pltpu.VMEM((ITEMS, PTS), F32),
            pltpu.VMEM((ITEMS, PTS), F32),
            pltpu.VMEM((128, 128), F32),
            pltpu.VMEM((PLANE - 1, 4, 128), F32),
            pltpu.VMEM((PLANE, 4, 128), F32),
            pltpu.VMEM((NX, ROWS + 32, 128), F32),
            pltpu.VMEM((NX, ROWS + 32, 128), F32),
            pltpu.VMEM((NX, ROWS + 32, 128), F32),
            pltpu.VMEM((NX - 1, ROWS + 32, 128), F32),
            pltpu.VMEM((PLANE - 1, 1, 128), F32),
            pltpu.VMEM((PLANE, 1, 128), F32),
            pltpu.VMEM((8, 256), F32),
            pltpu.VMEM((NR, 8, 256), F32),
            dma((len(arguments),)),
        ]
        + [dma, dma, dma, dma((NX,))]
        + [dma] * 6,
        compiler_params=pltpu.CompilerParams(
            collective_id=0, has_side_effects=True, vmem_limit_bytes=60 * 2**20
        ),
        name="collocate",
    )(*arguments)


def solution(mesh):
    spread = ("row", "col", "basis")
    return jax.shard_map(
        body,
        mesh=mesh,
        in_specs=(
            P(spread, None, None),
            P(spread, None),
            P(spread),
            P(spread),
            P(),
            P(),
            P(),
            P(spread, None),
            P(spread, None, None),
        ),
        out_specs=P(spread, None),
        check_vma=False,
    )
```

```python
import itertools

import jax
import jax.numpy as jnp
from jax import lax
from jax.experimental import pallas as pl
from jax.experimental.pallas import tpu as pltpu
from jax.sharding import PartitionSpec as P

MESH = pl.DeviceIdType.MESH
F32 = jnp.float32
BF16 = jnp.bfloat16

EDGE = 16
HALF = (EDGE - 1) / 2.0
PTS = EDGE**3
BS = 128
ITEMS = 8
NR, NC, NZ = 8, 8, 12
NX = NR // 2
PLANE = NC * NZ
BATCH = 24
GROUP = 24
OWN = NC * GROUP
SUB = 43
TARGET = SUB
CORNER = 48
ROWS = 56
NT = (((1,), (1,)), ((), ()))
CORNERS = tuple(
    ((c // 4) * 15 * EDGE + (c // 2 % 2) * 15) * EDGE + (c % 2) * 15 for c in range(8)
)


def far(step, size):
    return min(step, size - step)


PLANE_STEPS = sorted(
    (s for s in itertools.product(range(NC), range(NZ)) if any(s)),
    key=lambda s: -(far(s[0], NC) + far(s[1], NZ)),
)
ROW_STEPS = ((2, 1), (2, 0), (1, 1), (3, 1), (1, 0), (3, 0), (0, 1))


def lanes(shape):
    return lax.broadcasted_iota(jnp.int32, shape, len(shape) - 1)


def rows(shape):
    return lax.broadcasted_iota(jnp.int32, shape, len(shape) - 2)


def roll(x, shift):
    shift %= x.shape[-1]
    return x if shift == 0 else pltpu.roll(x, shift, x.ndim - 1)


def kernel(
    pairs_hbm,
    slot_hbm,
    tag_hbm,
    levels_hbm,
    cen_hbm,
    exp_hbm,
    block_hbm,
    refs_hbm,
    cell_hbm,
    out_ref,
    pairs_ref,
    slot_ref,
    tag_ref,
    levels_ref,
    cen_ref,
    exp_ref,
    block_ref,
    refs_ref,
    cell_ref,
    colx_ref,
    colyz_ref,
    rowx_ref,
    rowyz_ref,
    dens_ref,
    side_ref,
    bricks_ref,
    a_out,
    a_got,
    r_out,
    r_got,
    b_out,
    b_got,
    c_out,
    c_got,
    load_sem,
    a_send,
    a_recv,
    r_send,
    r_recv,
    b_send,
    b_recv,
    c_send,
    c_recv,
):
    loads = [
        pltpu.make_async_copy(source, into, load_sem.at[n])
        for n, (source, into) in enumerate(
            (
                (pairs_hbm, pairs_ref),
                (slot_hbm, slot_ref),
                (tag_hbm, tag_ref),
                (levels_hbm, levels_ref),
                (cen_hbm, cen_ref),
                (exp_hbm, exp_ref),
                (block_hbm, block_ref),
                (refs_hbm, refs_ref),
                (cell_hbm, cell_ref),
            )
        )
    ]
    r, y, z = (lax.axis_index(a) for a in ("row", "col", "basis"))
    ys = [lax.rem(y + n, NC) for n in range(NC)]
    zs = [lax.rem(z + n, NZ) for n in range(NZ)]
    x, core = r // 2, lax.rem(r, 2)
    xs = [lax.rem(x + n, NX) * 2 for n in range(NX)]
    cores = [core, 1 - core]
    row_of = [xs[dx] + cores[dc] for dx, dc in ROW_STEPS]
    me = y * NZ + z

    barrier = pltpu.get_barrier_semaphore()

    def entered(*device):
        pl.semaphore_signal(barrier, inc=1, device_id=device, device_id_type=MESH)

    for dy, dz in PLANE_STEPS[:BATCH]:
        entered(r, ys[dy], zs[dz])
    for load in loads:
        load.start()
    for dy, dz in PLANE_STEPS[BATCH:]:
        entered(r, ys[dy], zs[dz])
    for other in row_of:
        entered(other, y, z)

    step16 = rows((EDGE, BS)).astype(F32) - HALF
    lane256 = lanes((1, EDGE * EDGE))
    step_y = (lane256 // EDGE).astype(F32) - HALF
    step_z = (lane256 % EDGE).astype(F32) - HALF
    lane = lanes((ITEMS, 128))
    for load in loads:
        load.wait()

    numbers = jnp.zeros((ITEMS, 128), F32)
    spacings, params, row_xs = [], [], []
    for k in range(ITEMS):
        first, second = pairs_ref[0, k], pairs_ref[1, k]
        group, tag = slot_ref[k], tag_ref[k]
        spacing = jnp.where(levels_ref[group * GROUP + tag] == 0, 0.2, 0.1).astype(F32)
        spacings.append(spacing)
        place = (group & 7) * GROUP + tag
        number = (group >> 3) * OWN + (place & 1) * PLANE + (place >> 1)
        numbers = jnp.where(rows((ITEMS, 128)) == k, number.astype(F32), numbers)

        points = step16 * spacing
        rate = exp_ref[pl.ds(second, 1), :]
        middle = [cen_ref[d, pl.ds(second, 1), :] for d in range(3)]
        col_x, col_y, col_z = [jnp.exp(-rate * (points - m) ** 2) for m in middle]
        colx_ref[k] = col_x
        for n in range(EDGE):
            colyz_ref[k, n * EDGE : n * EDGE + EDGE, :] = col_y[n : n + 1] * col_z

        rate = exp_ref[pl.ds(first, 1), :]
        middle = [cen_ref[d, pl.ds(first, 1), :] for d in range(3)]
        row_xs.append(jnp.exp(-rate * (points - middle[0]) ** 2))
        params += [-rate, middle[1], middle[2]]
    columns = jnp.transpose(
        jnp.concatenate(params + [jnp.zeros((32 - 3 * ITEMS, BS), F32)], axis=0)
    )
    row_x = jnp.transpose(jnp.concatenate(row_xs, axis=0))
    for k in range(ITEMS):
        rowx_ref[k] = roll(row_x, -EDGE * k)
        decay, middle_y, middle_z = (columns[:, 3 * k + n : 3 * k + n + 1] for n in range(3))
        rowyz_ref[k] = jnp.exp(
            decay
            * (
                (step_y * spacings[k] - middle_y) ** 2
                + (step_z * spacings[k] - middle_z) ** 2
            )
        )

    def item(k, carry):
        block = block_ref[k]
        col_x = colx_ref[k]
        row_x = rowx_ref[k]
        for n in range(EDGE):
            col_values = (col_x[n : n + 1] * colyz_ref[k]).astype(BF16)
            product = lax.dot_general(block, col_values, NT, preferred_element_type=F32)
            weighted = product * rowyz_ref[k] * row_x[:, n : n + 1]
            dens_ref[pl.ds(k, 1), n * 256 : n * 256 + 256] = jnp.sum(
                weighted, axis=0, keepdims=True
            )
        return carry

    lax.fori_loop(0, ITEMS // 2, item, 0, unroll=True)
    lax.fori_loop(ITEMS // 2, ITEMS, item, 0, unroll=True)

    extra = jnp.where(lane == TARGET, numbers, 0.0)
    for c, q in enumerate(CORNERS):
        tile = dens_ref[:, q // 128 * 128 : q // 128 * 128 + 128]
        extra = jnp.where(lane == CORNER + c, roll(tile, CORNER + c - q), extra)
    lower = lane < 64

    def beside(x):
        return pltpu.roll(roll(x, 64), 4, 0)

    extra = jnp.where(lower, extra, beside(extra))
    point = (lane & 63) < SUB
    for t in range(PTS // 128):
        side_ref[:, t * 128 : t * 128 + 128] = beside(dens_ref[:, t * 128 : t * 128 + 128])
    tiles_y = [n * (NZ // 3) for n in ys]
    tiles_z = [n // 3 for n in zs]
    turns = [lax.rem(128 - SUB * lax.rem(n, 3), 128) for n in zs]

    def chunk(dy, dz):
        at = pl.ds(pl.multiple_of((tiles_y[dy] + tiles_z[dz]) * 128, 128), 128)
        value = jnp.where(
            lower,
            pltpu.roll(dens_ref[:, at], turns[dz], 1),
            pltpu.roll(side_ref[:, at], turns[dz], 1),
        )
        return jnp.where(point, value, extra)[:4]

    def plane_copies(made, out, got, send, recv):
        for begin in range(0, PLANE - 1, BATCH):
            batch = list(enumerate(PLANE_STEPS))[begin : begin + BATCH]
            for n, (dy, dz) in batch:
                out[n] = made(dy, dz)
            for n, (dy, dz) in batch:
                pltpu.make_async_remote_copy(
                    src_ref=out.at[n],
                    dst_ref=got.at[me],
                    send_sem=send,
                    recv_sem=recv,
                    device_id=(r, ys[dy], zs[dz]),
                    device_id_type=MESH,
                ).start()
        got[me] = made(0, 0)

    def arrived(ref, count, sem):
        whole = ref.at[pl.ds(0, count)]
        pltpu.make_async_copy(whole, whole, sem).wait()

    pl.semaphore_wait(barrier, PLANE + NR - 2)
    plane_copies(chunk, a_out, a_got, a_send, a_recv)
    arrived(a_got, PLANE - 1, a_recv)

    turned = jnp.transpose(
        jnp.concatenate([a_got[a] for a in range(PLANE)], axis=0)
    )
    values = jnp.concatenate([turned[:ROWS], turned[64 : 64 + ROWS]], axis=1)
    high = values.astype(BF16)
    low = (values - high.astype(F32)).astype(BF16)
    left = jnp.concatenate([high, low], axis=0)
    wanted = values[TARGET : TARGET + 1, :]
    count = rows((128, PLANE * ITEMS)).astype(F32)
    count2 = jnp.where(count < 64.0, count + 128.0, count + 64.0)
    half = lanes((32, 128)) < 64

    def table(row):
        here = wanted - (row * OWN).astype(F32)
        parts = []
        for at in (count, count2):
            right = jnp.where(at == here, 1.0, 0.0).astype(BF16)
            both = lax.dot_general(left, right, NT, preferred_element_type=F32)
            parts.append(both[:ROWS] + both[ROWS:])
        whole, mixed = parts
        mixed = jnp.concatenate([mixed, jnp.zeros((64 - ROWS, 128), F32)], axis=0)
        return jnp.concatenate([whole, jnp.where(half, mixed[:32], mixed[32:])], axis=0)

    for n, other in enumerate(row_of):
        r_out[n] = table(other)
        pltpu.make_async_remote_copy(
            src_ref=r_out.at[n],
            dst_ref=r_got.at[n],
            send_sem=r_send,
            recv_sem=r_recv,
            device_id=(other, y, z),
            device_id_type=MESH,
        ).start()
    total = table(r)
    arrived(r_got, NR - 1, r_recv)
    for n in range(NR - 1):
        total = total + r_got[n]
    whole, mixed = total[:ROWS], total[ROWS:]
    mixed = jnp.concatenate([mixed, roll(mixed, 64)], axis=0)

    c_out[:, :128] = whole[CORNER : CORNER + 8]
    c_out[:, 128:] = mixed[CORNER : CORNER + 8]
    for other in row_of:
        pltpu.make_async_remote_copy(
            src_ref=c_out,
            dst_ref=c_got.at[r],
            send_sem=c_send,
            recv_sem=c_recv,
            device_id=(other, y, z),
            device_id_type=MESH,
        ).start()
    c_got[r] = c_out[...]

    whole = jnp.concatenate([whole, jnp.zeros((64 - ROWS, 128), F32)], axis=0)
    second = jnp.where(lanes((64, 128)) < 32, roll(whole, 32), roll(mixed, 32))
    bricks_ref[...] = jnp.transpose(jnp.concatenate([whole, second], axis=0))

    def own_points(dy, dz):
        return bricks_ref[pl.ds(ys[dy] * NZ + zs[dz], 1), :]

    plane_copies(own_points, b_out, b_got, b_send, b_recv)

    arrived(c_got, NR - 1, c_recv)
    kept, added = [], []
    for b in range(2):
        means = []
        for h in range(2):
            ref = refs_ref[b, :, h * 128 : h * 128 + 128]
            corner, brick = ref & 7, ref >> 3
            source = ((brick >> 6) * 11) >> 5
            place = brick - source * OWN
            place = (place >> 1) + (place & 1) * PLANE
            at = place & 127
            which = (source * 2 + (place >> 7)) * 8 + corner
            found = jnp.zeros((8, 128), F32)
            for n in range(NR):
                for part in range(2):
                    for c in range(8):
                        line = jnp.broadcast_to(
                            c_got[n, c : c + 1, part * 128 : part * 128 + 128], (8, 128)
                        )
                        here = jnp.take_along_axis(line, at, axis=1)
                        found = jnp.where(which == (n * 2 + part) * 8 + c, here, found)
            means.append(jnp.sum(found, axis=0, keepdims=True) * 0.0625)
        mean = jnp.concatenate(means, axis=1)
        cell = cell_ref[b : b + 1, :]
        upper = rows((32, 256)) == (cell >> 7)
        coarse = mean.astype(BF16).astype(F32)
        weights = jnp.concatenate(
            [
                jnp.where(upper, coarse, 0.0),
                jnp.where(upper, mean - coarse, 0.0),
                jnp.where(upper, 0.5, 0.0),
            ],
            axis=0,
        ).astype(BF16)
        spots = jnp.where(rows((128, 256)) == (cell & 127), 1.0, 0.0).astype(BF16)
        spread = lax.dot_general(weights, spots, NT, preferred_element_type=F32)
        added.append(spread[:32] + spread[32:64])
        kept.append(1.0 - spread[64:])

    arrived(b_got, PLANE - 1, b_recv)
    lane = lanes((1, 128))
    for b in range(2):
        for t in range(PTS // 128):
            thirds = [roll(b_got[3 * t + m], SUB * m - 64 * b) for m in range(3)]
            value = jnp.where(
                lane < SUB, thirds[0], jnp.where(lane < 2 * SUB, thirds[1], thirds[2])
            )
            out_ref[b : b + 1, t * 128 : t * 128 + 128] = (
                value * kept[b][t : t + 1] + added[b][t : t + 1]
            )
    arrived(a_out, PLANE - 1, a_send)
    arrived(r_out, NR - 1, r_send)
    arrived(b_out, PLANE - 1, b_send)
    arrived(c_got, NR - 1, c_send)


def body(
    block_data, item_pairs, dest_slot, brick_tag, centres, exponents, levels, cell_pos, corner_refs
):
    arguments = (
        item_pairs.T,
        dest_slot,
        brick_tag,
        levels,
        centres.transpose(1, 0, 2),
        exponents,
        block_data,
        corner_refs.transpose(0, 2, 1),
        cell_pos,
    )
    places = [pltpu.SMEM] * 4 + [pltpu.VMEM] * 5
    dma = pltpu.SemaphoreType.DMA
    return pl.pallas_call(
        kernel,
        out_shape=pltpu.VMEM((2, PTS), F32),
        in_specs=[pl.BlockSpec(memory_space=pltpu.HBM)] * len(arguments),
        out_specs=pl.BlockSpec(memory_space=pltpu.VMEM),
        scratch_shapes=[place(a.shape, a.dtype) for place, a in zip(places, arguments)]
        + [
            pltpu.VMEM((ITEMS, EDGE, BS), F32),
            pltpu.VMEM((ITEMS, EDGE * EDGE, BS), F32),
            pltpu.VMEM((ITEMS, BS, 128), F32),
            pltpu.VMEM((ITEMS, BS, EDGE * EDGE), F32),
            pltpu.VMEM((ITEMS, PTS), F32),
            pltpu.VMEM((ITEMS, PTS), F32),
            pltpu.VMEM((128, 128), F32),
            pltpu.VMEM((PLANE - 1, 4, 128), F32),
            pltpu.VMEM((PLANE, 4, 128), F32),
            pltpu.VMEM((NR - 1, ROWS + 32, 128), F32),
            pltpu.VMEM((NR - 1, ROWS + 32, 128), F32),
            pltpu.VMEM((PLANE - 1, 1, 128), F32),
            pltpu.VMEM((PLANE, 1, 128), F32),
            pltpu.VMEM((8, 256), F32),
            pltpu.VMEM((NR, 8, 256), F32),
            dma((len(arguments),)),
        ]
        + [dma] * 8,
        compiler_params=pltpu.CompilerParams(
            collective_id=0, has_side_effects=True, vmem_limit_bytes=60 * 2**20
        ),
        name="collocate",
    )(*arguments)


def solution(mesh):
    spread = ("row", "col", "basis")
    return jax.shard_map(
        body,
        mesh=mesh,
        in_specs=(
            P(spread, None, None),
            P(spread, None),
            P(spread),
            P(spread),
            P(),
            P(),
            P(),
            P(spread, None),
            P(spread, None, None),
        ),
        out_specs=P(spread, None),
        check_vma=False,
    )
```
